512 devices in a mesh: dp: 512 (over z, y, x, core).
Axes of the slice: x: 4, y: 4, z: 16, core: 2. Of those that a mesh axis runs over, the one named last changes fastest.
Arguments:
- attn_out: bfloat16 [65536, 1024], P('dp'), may hold values from -24 to 24
- grad_out: bfloat16 [65536, 1024], P('dp'), may hold values from -6 to 6
- w_out: bfloat16 [1024, 1024], replicated, may hold values from -0.1875 to 0.1875
- codes_m: int32 [512, 2048], P('dp'), may hold values from 0 to 254
- codes_v: int32 [512, 2048], P('dp'), may hold values from 16 to 255
- scale_m: float32 [512], P('dp'), may hold values from 0.0002 to 0.002
- scale_v: float32 [512], P('dp'), may hold values from 1e-07 to 1e-06
- master: float32 [512, 2048], P('dp'), may hold values from -0.1875 to 0.1875
Outputs:
- d_attn: bfloat16 [65536, 1024], P('dp')
- m_unit: float32 [512, 2048], P('dp')
- v_unit: float32 [512, 2048], P('dp')
- new_master: float32 [512, 2048], P('dp')
The draws below stay inside these ranges and needn't reach their ends.
All inputs are finite; a program needn't handle non-finite values.
Results may differ from the reference program's by a relative error of at most 0.0013.
Values sent between devices are 32-bit elements; how exact they have to be, the bound alone decides.
A program may use at most 64 MiB of HBM per device.

```python
import math
import jax
import jax.numpy as jnp
from jax import lax

HEADS = 16
HEAD_DIM = 64
FEAT = 1024
TOK_DEV = 128
BLOCK = 2048
STEP = 100
HW = 1024
TOKENS = 65536
NBLK = 512
N_DP = 512


def plant(result, stream_key, smallest, high):
    extent = result.shape
    place = [jax.random.randint(jax.random.fold_in(stream_key, axis), (), 0, extent[axis]) for axis in range(len(extent))]
    result = result.at[tuple(place)].set(smallest)
    longest = extent.index(max(extent))
    place[longest] = (place[longest] + 1) % extent[longest]
    return result.at[tuple(place)].set(high)


def strengthened(array, key, source, target, blocks, factor):
    def block_of(position):
        return (jnp.arange(array.shape[position]) // (array.shape[position] // blocks)).reshape((-1,) + (1,) * (array.ndim - 1 - position))

    one_side = jax.random.permutation(key, blocks)[block_of(target)]
    second = (block_of(target) + blocks // 2) % blocks
    return jnp.where((block_of(source) == one_side) | (block_of(source) == second), factor * array, array)


def block_levels(own_key, shape, pieces, smallest, high):
    gain, own = 1.0, jax.random.fold_in(own_key, 6)
    for axis_at, parts in pieces:
        heights = jnp.exp(jax.random.uniform(jax.random.fold_in(own, axis_at), (parts,), jnp.float32, smallest / len(pieces), high / len(pieces)))
        gain = gain * jnp.repeat(heights, shape[axis_at] // parts).reshape([-1 if axis == axis_at else 1 for axis in range(len(shape))])
    return gain


def gaussian(own_key, dims, deviation, reach, shards=(), dtype=jnp.bfloat16):
    array = jax.random.normal(own_key, dims, jnp.float32) * deviation
    if len(shards) > 0:
        array = block_levels(own_key, dims, shards, -0.22, 0.18) * array
    return jnp.clip(array, min=-reach, max=reach).astype(dtype)


def gaussian_with(stream_key, dims, scale, bound, split, heavy, kind=jnp.bfloat16):
    entries = scale * jax.random.normal(stream_key, dims, jnp.float32)
    if split:
        entries = entries * block_levels(stream_key, dims, split, -0.22, 0.18)
    return jnp.clip(strengthened(entries, jax.random.fold_in(stream_key, 3), *heavy), -bound, bound).astype(kind)


def setup_inputs(seed: int = 0) -> dict:
    splits = jax.random.split(jax.random.key(seed), 9)
    return {
        "attn_out": gaussian_with(splits[0], (TOKENS, HW), 1.0, 24.0, ((0, 512),), (0, 1, 512, 6.0)),
        "grad_out": gaussian(splits[1], (TOKENS, FEAT), 1.0, 6.0, ((0, 512),)),
        "w_out": gaussian(splits[2], (HW, FEAT), FEAT ** -0.5, 0.1875),
        "codes_m": plant(jax.random.randint(splits[3], (NBLK, BLOCK), 0, 255), jax.random.fold_in(splits[3], 1), 0, 254).astype(jnp.int32),
        "codes_v": plant(jax.random.randint(splits[4], (NBLK, BLOCK), 16, 256), jax.random.fold_in(splits[4], 1), 16, 255).astype(jnp.int32),
        "scale_m": jnp.clip(jnp.exp(math.log(0.002) - 2.3025852 * jax.random.uniform(splits[5], (NBLK,), jnp.float32) ** block_levels(splits[5], (NBLK,), ((0, 512),), -0.2, 0.2)), 0.0002, 0.002),
        "scale_v": jnp.clip(jnp.exp(math.log(9.999999974752427e-07) - 2.3025851 * jax.random.uniform(splits[6], (NBLK,), jnp.float32) ** block_levels(splits[6], (NBLK,), ((0, 512),), -0.2, 0.2)), 1.0000000116860974e-07, 9.999999974752427e-07),
        "master": gaussian(splits[7], (NBLK, BLOCK), HW ** -0.5, 0.1875, ((0, 512),), jnp.float32),
    }


def reference(attn_out, grad_out, w_out, codes_m, codes_v, scale_m, scale_v, master):
    d_attn = jnp.dot(grad_out, w_out.T, preferred_element_type=jnp.float32).astype(jnp.bfloat16)
    pieces_a = attn_out.reshape(N_DP, TOK_DEV, HEADS * HEAD_DIM)
    pieces_d = grad_out.reshape(N_DP, TOK_DEV, FEAT)

    def accumulate(carry, pair):
        return (carry + jnp.dot(pair[0].T, pair[1], preferred_element_type=jnp.float32), None)
    start = jnp.zeros((HEADS * HEAD_DIM, FEAT), jnp.float32)
    gradient, unused = lax.scan(accumulate, start, (pieces_a, pieces_d))
    gradient = gradient.reshape(NBLK, BLOCK)
    clip = jnp.minimum(1.0, 1.0 / jnp.sqrt(jnp.sum(gradient * gradient) + 1e-12))
    m_old = scale_m[:, None] * (codes_m.astype(jnp.float32) - 127.0) / 127.0
    ratio_v = codes_v.astype(jnp.float32) / 255.0
    v_old = scale_v[:, None] * ratio_v * ratio_v
    clipped = clip * gradient
    m_new = 0.9 * m_old + 0.1 * clipped
    v_new = 0.95 * v_old + 0.05 * clipped * clipped
    step = m_new / (1.0 - 0.9 ** STEP) / (jnp.sqrt(v_new / (1.0 - 0.95 ** STEP)) + 1e-08)
    new_master = master - 0.01 * (step + 0.1 * master)
    return (d_attn, m_new / scale_m[:, None], v_new / scale_v[:, None], new_master)
```

```python
import functools

import jax
import jax.numpy as jnp
from jax import lax
from jax.experimental import pallas as pl
from jax.experimental.pallas import tpu as pltpu
from jax.sharding import PartitionSpec as P

STEP = 100
NX, NY, NZ = 4, 4, 16
PLANE = NX * NY * 2
PARTS = 1
UNITS = 2 * PARTS
WIDTH = 1024 // UNITS
TOK = 128
MESH = pl.DeviceIdType.MESH


def kernel(
    a_hbm, g_hbm, w_hbm, cm_hbm, cv_hbm, sm_ref, sv_ref, ma_hbm,
    d_ref, mu_ref, vu_ref, nm_ref,
    a_in, g_in, w_in, cm, cv, ma,
    at_send, at_recv, g_send, g_recv, at_all, g_all,
    prod, first, second, zsend, zrecv, plane_sum, ring_sum,
    in_sem, core_s, core_r, first_s, first_r, second_s, second_r, z_s, z_r, p_s, p_r, q_s, q_r,
):
    me = lax.axis_index("dp")
    core = lax.rem(me, 2)
    x = lax.rem(me // 2, NX)
    y = lax.rem(me // (2 * NX), NY)
    z = me // PLANE
    q = lax.rem(me, PLANE)

    def device(z_, y_, x_, c_):
        return ((z_ * NY + y_) * NX + x_) * 2 + c_

    loads = []
    for i, (src, dst) in enumerate(
        ((a_hbm, a_in), (g_hbm, g_in), (w_hbm, w_in), (cm_hbm, cm), (cv_hbm, cv), (ma_hbm, ma))
    ):
        copy = pltpu.make_async_copy(src, dst, in_sem.at[i])
        copy.start()
        loads.append(copy)

    barrier = pltpu.get_barrier_semaphore()

    def greet_z(k, _):
        other = lax.rem(z + k, NZ)
        for c_ in range(2):
            pl.semaphore_signal(
                barrier, inc=1, device_id=(device(other, y, x, c_),), device_id_type=MESH
            )
        return 0

    def greet_plane(k, _):
        pl.semaphore_signal(
            barrier, inc=1, device_id=(z * PLANE + lax.rem(q + k, PLANE),), device_id_type=MESH
        )
        return 0

    lax.fori_loop(1, NZ, greet_z, 0)
    lax.fori_loop(1, PLANE, greet_plane, 0)

    row = lax.broadcasted_iota(jnp.int32, (512, 512), 0)
    column = lax.broadcasted_iota(jnp.int32, (512, 512), 1)
    wanted = ((row >> 2) & 7) * 64 + ((row >> 5) & 3) * 16 + ((row >> 7) & 3) * 4 + (row & 3)
    order = jnp.where(wanted == column, 1.0, 0.0).astype(jnp.bfloat16)
    loads[0].wait()
    loads[1].wait()
    for u in range(UNITS):
        piece = g_in[:, u * WIDTH : (u + 1) * WIDTH]
        g_send[u] = piece.astype(jnp.float32)
        g_all[u, 0:TOK, :] = piece

    def rows_of(c_):
        half = a_in[:, pl.ds(pl.multiple_of(c_ * 512, 512), 512)]
        return lax.dot_general(
            order, half, (((1,), (1,)), ((), ())), preferred_element_type=jnp.float32
        )

    at_send[...] = rows_of(1 - core)
    at_all[:, 0:TOK] = rows_of(core).astype(jnp.bfloat16)

    pl.semaphore_wait(barrier, (NZ - 1) * 2 + PLANE - 1)

    def push(src, dst, s, r, target):
        copy = pltpu.make_async_remote_copy(
            src_ref=src, dst_ref=dst, send_sem=s, recv_sem=r,
            device_id=(target,), device_id_type=MESH,
        )
        copy.start()
        return copy

    twin = device(z, y, x, 1 - core)
    across = [push(at_send, at_recv, core_s.at[UNITS], core_r.at[UNITS], twin)]
    for u in range(UNITS):
        across.append(push(g_send.at[u], g_recv.at[u], core_s.at[u], core_r.at[u], twin))
    across[0].wait_recv()
    at_all[:, TOK : 2 * TOK] = at_recv[...].astype(jnp.bfloat16)

    def block(u, k):
        if u % 2 == 0:
            rows = at_all[pl.ds(pl.multiple_of(k * 128, 128), 128), :]
        else:
            rows = jnp.concatenate(
                [at_all[pl.ds(pl.multiple_of(i * 128 + k * 32, 32), 32), :] for i in range(4)],
                axis=0,
            )
        return jnp.dot(rows, g_all[u], preferred_element_type=jnp.float32)

    def places(u):
        return (x, y) if u % 2 == 0 else (y, x)

    def along(u, stage, k):
        if (u % 2 == 0) == (stage == 0):
            return device(z, y, k, core)
        return device(z, k, x, core)

    sent_first = {}
    for u in range(UNITS):
        across[u + 1].wait_recv()
        g_all[u, TOK : 2 * TOK, :] = g_recv[u].astype(jnp.bfloat16)
    for s in range(PARTS):
        for hop in (2, 1, 3):
            for u in (2 * s, 2 * s + 1):
                k = lax.rem(places(u)[0] + hop, 4)
                prod[u, hop] = block(u, k)
                sent_first[u, hop] = push(
                    prod.at[u, hop], first.at[u, hop - 1],
                    first_s.at[u, hop - 1], first_r.at[u, hop - 1], along(u, 0, k),
                )
        for u in (2 * s, 2 * s + 1):
            prod[u, 0] = block(u, places(u)[0])

    loads[2].wait()
    for h in range(4):
        d_ref[:, h * 256 : (h + 1) * 256] = lax.dot_general(
            g_in[...], w_in[h * 256 : (h + 1) * 256, :], (((1,), (1,)), ((), ())),
            preferred_element_type=jnp.float32,
        ).astype(jnp.bfloat16)

    sent_second = {}
    for u in range(UNITS):
        for hop in (1, 3, 2):
            sent_first[u, hop].wait_recv()
        total = prod[u, 0] + first[u, 0] + first[u, 1] + first[u, 2]
        prod[u, 0] = total
        for hop in (2, 1, 3):
            k = lax.rem(places(u)[1] + hop, 4)
            sent_second[u, hop] = push(
                prod.at[u, 0, pl.ds(pl.multiple_of(k * 32, 32), 32)], second.at[u, hop - 1],
                second_s.at[u, hop - 1], second_r.at[u, hop - 1], along(u, 1, k),
            )

    for u in range(UNITS):
        for hop in (1, 3, 2):
            sent_second[u, hop].wait_recv()
        mine = prod[u, 0, pl.ds(pl.multiple_of(places(u)[1] * 32, 32), 32)]
        total = mine + second[u, 0] + second[u, 1] + second[u, 2]
        for k in range(16):
            zsend[k, :, u * WIDTH : (u + 1) * WIDTH] = total[2 * k : 2 * k + 2]

    def z_copy(k):
        z_, c_ = 8 * core + k // 2, lax.rem(k, 2)
        return z_, c_, pltpu.make_async_remote_copy(
            src_ref=zsend.at[k], dst_ref=zrecv.at[z], send_sem=z_s, recv_sem=z_r,
            device_id=(device(z_, y, x, c_),), device_id_type=MESH,
        )

    def z_start(i, _):
        k = lax.rem(i + 2 * z + 8, 16)
        z_, c_, copy = z_copy(k)
        mine = jnp.logical_and(z_ == z, c_ == core)

        @pl.when(jnp.logical_not(mine))
        def _():
            copy.start()

        @pl.when(mine)
        def _():
            pltpu.make_async_copy(zsend.at[k], zrecv.at[z], z_r).start()

        return 0

    lax.fori_loop(0, 16, z_start, 0)
    pltpu.make_async_copy(zrecv, zrecv, z_r).wait()
    gradient = zrecv[0]
    for k in range(1, NZ):
        gradient = gradient + zrecv[k]

    def spread(slots, slot, count, target, s, r, value):
        slots[slot] = jnp.full((1, 128), value, jnp.float32)

        def start(k, _):
            pltpu.make_async_remote_copy(
                src_ref=slots.at[slot], dst_ref=slots.at[slot], send_sem=s, recv_sem=r,
                device_id=(target(k),), device_id_type=MESH,
            ).start()
            return 0

        lax.fori_loop(1, count, start, 0)
        arrived = slots.at[pl.ds(0, count - 1)]
        pltpu.make_async_copy(arrived, arrived, r).wait()
        return jnp.sum(slots[...], axis=0)

    square = jnp.sum(gradient * gradient)
    square = spread(
        plane_sum, q, PLANE, lambda k: z * PLANE + lax.rem(q + k, PLANE), p_s, p_r, square
    )[0, 0]
    square = spread(
        ring_sum, z, NZ, lambda k: lax.rem(z + k, NZ) * PLANE + q, q_s, q_r, square
    )
    clip = jnp.minimum(1.0, 1.0 / jnp.sqrt(square[:, 0:1] + 1e-12))

    for load in loads[3:]:
        load.wait()
    scale_m, scale_v = sm_ref[0], sv_ref[0]
    for p in range(2):
        part = slice(p * 1024, (p + 1) * 1024)
        m_old = scale_m * (cm[:, part].astype(jnp.float32) - 127.0) / 127.0
        ratio_v = cv[:, part].astype(jnp.float32) / 255.0
        v_old = scale_v * ratio_v * ratio_v
        clipped = clip * gradient[p : p + 1, :]
        m_new = 0.9 * m_old + 0.1 * clipped
        v_new = 0.95 * v_old + 0.05 * clipped * clipped
        update = m_new / (1.0 - 0.9**STEP) / (jnp.sqrt(v_new / (1.0 - 0.95**STEP)) + 1e-08)
        nm_ref[:, part] = ma[:, part] - 0.01 * (update + 0.1 * ma[:, part])
        mu_ref[:, part] = m_new / scale_m
        vu_ref[:, part] = v_new / scale_v

    for copy in across:
        copy.wait_send()
    for copy in (*sent_first.values(), *sent_second.values()):
        copy.wait_send()
    away = jnp.logical_not((z // 8) == core)

    @pl.when(away)
    def _():
        pltpu.make_async_copy(zsend, zsend, z_s).wait()

    @pl.when(jnp.logical_not(away))
    def _():
        left = zsend.at[pl.ds(0, 15)]
        pltpu.make_async_copy(left, left, z_s).wait()

    for slots, count, s in ((plane_sum, PLANE, p_s), (ring_sum, NZ, q_s)):
        left = slots.at[pl.ds(0, count - 1)]
        pltpu.make_async_copy(left, left, s).wait()


def local(attn_out, grad_out, w_out, codes_m, codes_v, scale_m, scale_v, master):
    f32, bf16 = jnp.float32, jnp.bfloat16
    vmem, dma = pltpu.VMEM, pltpu.SemaphoreType.DMA
    block = jax.ShapeDtypeStruct((1, 2048), f32)
    anywhere = pl.BlockSpec(memory_space=pl.ANY)
    scalar = pl.BlockSpec(memory_space=pltpu.SMEM)
    return pl.pallas_call(
        kernel,
        out_shape=(jax.ShapeDtypeStruct((TOK, 1024), bf16), block, block, block),
        in_specs=[anywhere] * 5 + [scalar] * 2 + [anywhere],
        out_specs=tuple([pl.BlockSpec(memory_space=pltpu.VMEM)] * 4),
        scratch_shapes=[
            vmem((TOK, 1024), bf16),
            vmem((TOK, 1024), bf16),
            vmem((1024, 1024), bf16),
            vmem((1, 2048), jnp.int32),
            vmem((1, 2048), jnp.int32),
            vmem((1, 2048), f32),
            vmem((512, TOK), f32),
            vmem((512, TOK), f32),
            vmem((UNITS, TOK, WIDTH), f32),
            vmem((UNITS, TOK, WIDTH), f32),
            vmem((512, 2 * TOK), bf16),
            vmem((UNITS, 2 * TOK, WIDTH), bf16),
            vmem((UNITS, 4, 128, WIDTH), f32),
            vmem((UNITS, 3, 128, WIDTH), f32),
            vmem((UNITS, 3, 32, WIDTH), f32),
            vmem((16, 2, 1024), f32),
            vmem((NZ, 2, 1024), f32),
            vmem((PLANE, 1, 128), f32),
            vmem((NZ, 1, 128), f32),
            dma((6,)),
            dma((UNITS + 1,)),
            dma((UNITS + 1,)),
            dma((UNITS, 3)),
            dma((UNITS, 3)),
            dma((UNITS, 3)),
            dma((UNITS, 3)),
            dma,
            dma,
            dma,
            dma,
            dma,
            dma,
        ],
        compiler_params=pltpu.CompilerParams(
            collective_id=0, has_side_effects=True, vmem_limit_bytes=40 * 2**20
        ),
        cost_estimate=pl.CostEstimate(
            flops=2 * 2 * TOK * 1024 * 1024, bytes_accessed=3 * 2**20, transcendentals=4096
        ),
    )(attn_out, grad_out, w_out, codes_m, codes_v, scale_m, scale_v, master)


def solution(mesh):
    in_specs = (
        P("dp", None),
        P("dp", None),
        P(),
        P("dp", None),
        P("dp", None),
        P("dp"),
        P("dp"),
        P("dp", None),
    )
    out_specs = (P("dp", None), P("dp", None), P("dp", None), P("dp", None))
    return jax.shard_map(local, mesh=mesh, in_specs=in_specs, out_specs=out_specs, check_vma=False)
```

```python
import functools

import jax
import jax.numpy as jnp
from jax import lax
from jax.experimental import pallas as pl
from jax.experimental.pallas import tpu as pltpu
from jax.sharding import PartitionSpec as P

STEP = 100
NX, NY, NZ = 4, 4, 16
PLANE = NX * NY * 2
TOK = 128
WIDTHS = (256, 256, 256, 256)
STARTS = tuple(sum(WIDTHS[:u]) for u in range(4))
PLAIN, PAIRED = (0, 1), (2, 3)
WIDE0, WIDE1 = WIDTHS[0] + WIDTHS[1], WIDTHS[2] + WIDTHS[3]
HOPS = (2, 1, 3)
MESH = pl.DeviceIdType.MESH


def push(src, dst, s, r, target):
    copy = pltpu.make_async_remote_copy(
        src_ref=src, dst_ref=dst, send_sem=s, recv_sem=r, device_id=(target,), device_id_type=MESH
    )
    copy.start()
    return copy


def kernel(
    a_hbm, g_hbm, w_hbm, cm_hbm, cv_hbm, ma_hbm,
    d_ref, gradient_ref, square_ref, cm_ref, cv_ref, ma_ref,
    a_in, g_in, w_in,
    at_send, at_recv, g_send, g_recv, at_all, g_all,
    prod0, prod1, prod2, prod3, pair, pair_in, first_in, first_in_p, second_in, second_in_p,
    zsend0, zrecv0, zsend1, zrecv1, plane_sum, ring_sum,
    in_sem, core_s, core_r, pair_s, pair_r, first_s, first_r, second_s, second_r,
    z0_s, z0_r, z1_s, z1_r, p_s, p_r, q_s, q_r,
):
    me = lax.axis_index("dp")
    core = lax.rem(me, 2)
    x = lax.rem(me // 2, NX)
    y = lax.rem(me // (2 * NX), NY)
    z = me // PLANE
    q = lax.rem(me, PLANE)
    parity = lax.rem(z, 2)

    def device(z_, y_, x_, c_):
        return ((z_ * NY + y_) * NX + x_) * 2 + c_

    loads = []
    for i, (src, dst) in enumerate(
        (
            (a_hbm, a_in), (g_hbm, g_in), (w_hbm, w_in),
            (cm_hbm, cm_ref), (cv_hbm, cv_ref), (ma_hbm, ma_ref),
        )
    ):
        copy = pltpu.make_async_copy(src, dst, in_sem.at[i])
        copy.start()
        loads.append(copy)

    barrier = pltpu.get_barrier_semaphore()

    def greet_z(k, _):
        other = lax.rem(z + k + 7, NZ)

        @pl.when(other != z)
        def _():
            for c_ in range(2):
                pl.semaphore_signal(
                    barrier, inc=1, device_id=(device(other, y, x, c_),), device_id_type=MESH
                )

        return 0

    def greet_plane(k, _):
        pl.semaphore_signal(
            barrier, inc=1, device_id=(z * PLANE + lax.rem(q + k, PLANE),), device_id_type=MESH
        )
        return 0

    lax.fori_loop(0, NZ, greet_z, 0)
    lax.fori_loop(1, PLANE, greet_plane, 0)

    row = lax.broadcasted_iota(jnp.int32, (512, 512), 0)
    column = lax.broadcasted_iota(jnp.int32, (512, 512), 1)
    wanted = (
        ((row >> 2) & 3) * 128
        + ((row >> 4) & 1) * 64
        + ((row >> 5) & 3) * 16
        + ((row >> 7) & 3) * 4
        + (row & 3)
    )
    order = jnp.where(wanted == column, 1.0, 0.0).astype(jnp.bfloat16)

    def rows_of(c_):
        half = a_in[:, pl.ds(pl.multiple_of(c_ * 512, 512), 512)]
        return lax.dot_general(
            order, half, (((1,), (1,)), ((), ())), preferred_element_type=jnp.float32
        )

    loads[0].wait()
    at_send[...] = rows_of(1 - core)
    loads[1].wait()
    for u in range(4):
        piece = g_in[:, STARTS[u] : STARTS[u] + 256]
        g_send[u] = piece.astype(jnp.float32)

    pl.semaphore_wait(barrier, (NZ - 1) * 2 + PLANE - 1)

    twin = device(z, y, x, 1 - core)
    across = {4: push(at_send, at_recv, core_s.at[4], core_r.at[4], twin)}
    for u in (*PAIRED, *PLAIN):
        across[u] = push(g_send.at[u], g_recv.at[u], core_s.at[u], core_r.at[u], twin)

    at_all[:, :, :, :, 0:TOK] = rows_of(core).astype(jnp.bfloat16).reshape(4, 4, 2, 16, TOK)
    for u in range(4):
        g_all[u, 0:TOK, :] = g_in[:, STARTS[u] : STARTS[u] + 256]
    across[4].wait_recv()
    at_all[:, :, :, :, TOK : 2 * TOK] = (
        at_recv[...].astype(jnp.bfloat16).reshape(4, 4, 2, 16, TOK)
    )

    def times(rows, u):
        return jnp.dot(rows, g_all[u], preferred_element_type=jnp.float32)

    def block(u, k):
        rows = at_all[k] if u % 2 == 0 else at_all[:, k]
        return times(rows.reshape(128, 2 * TOK), u).reshape(4, 32, WIDTHS[u])

    def block_of(u, k, parity_):
        rows = at_all[k, :, parity_] if u % 2 == 0 else at_all[:, k, parity_]
        return times(rows.reshape(64, 2 * TOK), u).reshape(4, 16, WIDTHS[u])

    def places(u):
        return (x, y) if u % 2 == 0 else (y, x)

    def along(u, stage, k):
        if (u % 2 == 0) == (stage == 0):
            return device(z, y, k, core)
        return device(z, k, x, core)

    prod = (prod0, prod1, prod2, prod3)
    step = 1 - 2 * parity
    mates = {
        2: device(lax.rem(z + step + NZ, NZ), y, x, core),
        3: device(lax.rem(z - step + NZ, NZ), y, x, core),
    }
    sent_pair, sent_first, sent_second = {}, {}, {}

    def send_first(u, hop):
        k = lax.rem(places(u)[0] + hop, 4)
        into = first_in if u in PLAIN else first_in_p
        sent_first[u, hop] = push(
            prod[u].at[hop], into.at[u % 2, hop - 1],
            first_s.at[u, hop - 1], first_r.at[u, hop - 1], along(u, 0, k),
        )

    for u in (*PAIRED, *PLAIN):
        across[u].wait_recv()
        g_all[u, TOK : 2 * TOK, :] = g_recv[u].astype(jnp.bfloat16)
    for hop in (*HOPS, 0):
        for u in PAIRED:
            k = lax.rem(places(u)[0] + hop, 4)
            pair[u - 2, hop] = block_of(u, k, 1 - parity)
            sent_pair[u, hop] = push(
                pair.at[u - 2, hop], pair_in.at[u - 2, hop],
                pair_s.at[u - 2, hop], pair_r.at[u - 2, hop], mates[u],
            )
        if hop:
            for u in PLAIN:
                prod[u][hop] = block(u, lax.rem(places(u)[0] + hop, 4))
                send_first(u, hop)
    for hop in (*HOPS, 0):
        for u in PAIRED:
            prod[u][hop] = block_of(u, lax.rem(places(u)[0] + hop, 4), parity)
    for u in PLAIN:
        prod[u][0] = block(u, places(u)[0])

    def cotangent(h):
        d_ref[:, h * 256 : (h + 1) * 256] = lax.dot_general(
            g_in[...], w_in[h * 256 : (h + 1) * 256, :], (((1,), (1,)), ((), ())),
            preferred_element_type=jnp.float32,
        ).astype(jnp.bfloat16)

    for hop in HOPS:
        for u in PAIRED:
            sent_pair[u, hop].wait_recv()
            prod[u][hop] = prod[u][hop] + pair_in[u - 2, hop]
            send_first(u, hop)

    loads[2].wait()
    for h in range(4):
        cotangent(h)

    def end_first(u):
        into = first_in if u in PLAIN else first_in_p
        if u in PAIRED:
            sent_pair[u, 0].wait_recv()
        for hop in (1, 3, 2):
            sent_first[u, hop].wait_recv()
        i = u % 2
        total = prod[u][0] + into[i, 0] + into[i, 1] + into[i, 2]
        if u in PAIRED:
            total = total + pair_in[u - 2, 0]
        prod[u][0] = total
        into = second_in if u in PLAIN else second_in_p
        for hop in HOPS:
            k = lax.rem(places(u)[1] + hop, 4)
            sent_second[u, hop] = push(
                prod[u].at[0, k], into.at[i, hop - 1],
                second_s.at[u, hop - 1], second_r.at[u, hop - 1], along(u, 1, k),
            )

    def end_second(u, zsend):
        into = second_in if u in PLAIN else second_in_p
        for hop in (1, 3, 2):
            sent_second[u, hop].wait_recv()
        i = u % 2
        total = prod[u][0, places(u)[1]] + into[i, 0] + into[i, 1] + into[i, 2]
        start = STARTS[u] - STARTS[u - i]
        for k in range(zsend.shape[0]):
            zsend[k, :, start : start + WIDTHS[u]] = total[2 * k : 2 * k + 2]

    def along_z(zsend, zrecv, s, r, slot, count, owner):
        def start(i, _):
            k, z_, c_ = owner(i)
            mine = jnp.logical_and(z_ == z, c_ == core)

            @pl.when(jnp.logical_not(mine))
            def _():
                push(zsend.at[k], zrecv.at[slot], s, r, device(z_, y, x, c_))

            @pl.when(mine)
            def _():
                pltpu.make_async_copy(zsend.at[k], zrecv.at[slot], r).start()

            return 0

        lax.fori_loop(0, count, start, 0)

    def owner0(i):
        near, c_ = lax.rem(z + 4 + i // 2, 8), lax.rem(i, 2)
        return lax.rem(near, 2) * 8 + (near // 2) * 2 + c_, 8 * core + near, c_

    def owner1(i):
        near, c_ = lax.rem(z // 2 + 2 + i // 2, 4), lax.rem(i, 2)
        return near * 2 + c_, 8 * core + 2 * near + parity, c_

    for u in PLAIN:
        end_first(u)
    for u in PAIRED:
        end_first(u)
    for u in PLAIN:
        end_second(u, zsend0)
    along_z(zsend0, zrecv0, z0_s, z0_r, z, 16, owner0)
    for u in PAIRED:
        end_second(u, zsend1)
    along_z(zsend1, zrecv1, z1_s, z1_r, z // 2, 8, owner1)

    def gather_z(zrecv, r):
        pltpu.make_async_copy(zrecv, zrecv, r).wait()
        total = zrecv[0]
        for k in range(1, zrecv.shape[0]):
            total = total + zrecv[k]
        return total

    plain = gather_z(zrecv0, z0_r)
    gradient_ref[:, 0:WIDE0] = plain
    paired = gather_z(zrecv1, z1_r)
    gradient_ref[:, WIDE0:1024] = paired

    def spread(slots, slot, count, target, s, r, value):
        slots[slot] = jnp.full((1, 128), value, jnp.float32)

        def start(k, _):
            push(slots.at[slot], slots.at[slot], s, r, target(k))
            return 0

        lax.fori_loop(1, count, start, 0)
        arrived = slots.at[pl.ds(0, count - 1)]
        pltpu.make_async_copy(arrived, arrived, r).wait()
        return jnp.sum(slots[...], axis=0)

    square = jnp.sum(plain * plain) + jnp.sum(paired * paired)
    square = spread(
        plane_sum, q, PLANE, lambda k: z * PLANE + lax.rem(q + k, PLANE), p_s, p_r, square
    )[0, 0]
    square_ref[...] = spread(
        ring_sum, z, NZ, lambda k: lax.rem(z + k + 7 + k // 9, NZ) * PLANE + q, q_s, q_r, square
    )

    for load in loads[3:]:
        load.wait()
    for sent in (across, sent_pair, sent_first, sent_second):
        for copy in sent.values():
            copy.wait_send()

    def left(buffer, count, s):
        gone = buffer.at[pl.ds(0, count)]
        pltpu.make_async_copy(gone, gone, s).wait()

    at_home = (z // 8) == core

    @pl.when(at_home)
    def _():
        left(zsend0, 15, z0_s)
        left(zsend1, 7, z1_s)

    @pl.when(jnp.logical_not(at_home))
    def _():
        left(zsend0, 16, z0_s)
        left(zsend1, 8, z1_s)

    left(plane_sum, PLANE - 1, p_s)
    left(ring_sum, NZ - 1, q_s)


def update_kernel(
    d_ref, gradient_ref, square_ref, cm, cv, ma, sm_ref, sv_ref,
    d_out, mu_out, vu_out, nm_out,
    mu, vu, nm, sem,
):
    stores = [
        pltpu.make_async_copy(src, dst, sem.at[i])
        for i, (src, dst) in enumerate(((d_ref, d_out), (mu, mu_out), (vu, vu_out), (nm, nm_out)))
    ]
    stores[0].start()
    clip = jnp.minimum(1.0, 1.0 / jnp.sqrt(square_ref[:, 0:1] + 1e-12))
    scale_m, scale_v = sm_ref[0], sv_ref[0]
    for p in range(2):
        part = slice(p * 1024, (p + 1) * 1024)
        m_old = scale_m * (cm[:, part].astype(jnp.float32) - 127.0) / 127.0
        ratio_v = cv[:, part].astype(jnp.float32) / 255.0
        v_old = scale_v * ratio_v * ratio_v
        clipped = clip * gradient_ref[p : p + 1, :]
        m_new = 0.9 * m_old + 0.1 * clipped
        v_new = 0.95 * v_old + 0.05 * clipped * clipped
        update = m_new / (1.0 - 0.9**STEP) / (jnp.sqrt(v_new / (1.0 - 0.95**STEP)) + 1e-08)
        nm[:, part] = ma[:, part] - 0.01 * (update + 0.1 * ma[:, part])
        mu[:, part] = m_new / scale_m
        vu[:, part] = v_new / scale_v
    for store in stores[1:]:
        store.start()
    for store in stores:
        store.wait()


def local(attn_out, grad_out, w_out, codes_m, codes_v, scale_m, scale_v, master):
    f32, bf16 = jnp.float32, jnp.bfloat16
    vmem, dma = pltpu.VMEM, pltpu.SemaphoreType.DMA
    shape = jax.ShapeDtypeStruct
    hbm = pl.BlockSpec(memory_space=pltpu.HBM)
    near = pl.BlockSpec(memory_space=pltpu.VMEM)
    scalar = pl.BlockSpec(memory_space=pltpu.SMEM)
    integers = shape((1, 2048), jnp.int32)
    block = shape((1, 2048), f32)
    near_by = pl.pallas_call(
        kernel,
        out_shape=(
            shape((TOK, 1024), bf16), shape((2, 1024), f32), shape((1, 128), f32),
            integers, integers, block,
        ),
        in_specs=[hbm] * 6,
        out_specs=(near,) * 6,
        scratch_shapes=[
            vmem((TOK, 1024), bf16),
            vmem((TOK, 1024), bf16),
            vmem((1024, 1024), bf16),
            vmem((512, TOK), f32),
            vmem((512, TOK), f32),
            vmem((4, TOK, 256), f32),
            vmem((4, TOK, 256), f32),
            vmem((4, 4, 2, 16, 2 * TOK), bf16),
            vmem((4, 2 * TOK, 256), bf16),
            vmem((4, 4, 32, WIDTHS[0]), f32),
            vmem((4, 4, 32, WIDTHS[1]), f32),
            vmem((4, 4, 16, WIDTHS[2]), f32),
            vmem((4, 4, 16, WIDTHS[3]), f32),
            vmem((2, 4, 4, 16, WIDTHS[2]), f32),
            vmem((2, 4, 4, 16, WIDTHS[2]), f32),
            vmem((2, 3, 4, 32, WIDTHS[0]), f32),
            vmem((2, 3, 4, 16, WIDTHS[2]), f32),
            vmem((2, 3, 32, WIDTHS[0]), f32),
            vmem((2, 3, 16, WIDTHS[2]), f32),
            vmem((16, 2, WIDE0), f32),
            vmem((16, 2, WIDE0), f32),
            vmem((8, 2, WIDE1), f32),
            vmem((8, 2, WIDE1), f32),
            vmem((PLANE, 1, 128), f32),
            vmem((NZ, 1, 128), f32),
            dma((6,)),
            dma((5,)),
            dma((5,)),
            dma((2, 4)),
            dma((2, 4)),
            dma((4, 3)),
            dma((4, 3)),
            dma((4, 3)),
            dma((4, 3)),
            *[dma] * 8,
        ],
        compiler_params=pltpu.CompilerParams(
            collective_id=0, has_side_effects=True, vmem_limit_bytes=60 * 2**20
        ),
        cost_estimate=pl.CostEstimate(
            flops=2 * 2 * TOK * 1024 * 1024, bytes_accessed=3 * 2**20, transcendentals=0
        ),
    )(attn_out, grad_out, w_out, codes_m, codes_v, master)
    return pl.pallas_call(
        update_kernel,
        out_shape=(shape((TOK, 1024), bf16), block, block, block),
        in_specs=[near] * 6 + [scalar] * 2,
        out_specs=(hbm,) * 4,
        scratch_shapes=[
            vmem((1, 2048), f32),
            vmem((1, 2048), f32),
            vmem((1, 2048), f32),
            dma((4,)),
        ],
        cost_estimate=pl.CostEstimate(flops=2048 * 30, bytes_accessed=2**19, transcendentals=4096),
    )(*near_by, scale_m, scale_v)


def solution(mesh):
    in_specs = (
        P("dp", None),
        P("dp", None),
        P(),
        P("dp", None),
        P("dp", None),
        P("dp"),
        P("dp"),
        P("dp", None),
    )
    out_specs = (P("dp", None), P("dp", None), P("dp", None), P("dp", None))
    return jax.shard_map(local, mesh=mesh, in_specs=in_specs, out_specs=out_specs, check_vma=False)
```

```python
import functools

import jax
import jax.numpy as jnp
from jax import lax
from jax.experimental import pallas as pl
from jax.experimental.pallas import tpu as pltpu
from jax.sharding import PartitionSpec as P

STEP = 100
NX, NY, NZ = 4, 4, 16
PLANE = NX * NY * 2
TOK = 128
WIDTHS = (256, 256, 256, 256)
STARTS = tuple(sum(WIDTHS[:u]) for u in range(4))
PLAIN, PAIRED = (0, 1), (2, 3)
WIDE0, WIDE1 = WIDTHS[0] + WIDTHS[1], WIDTHS[2] + WIDTHS[3]
HOPS = (2, 1, 3)
MESH = pl.DeviceIdType.MESH


def push(src, dst, s, r, target):
    copy = pltpu.make_async_remote_copy(
        src_ref=src, dst_ref=dst, send_sem=s, recv_sem=r, device_id=(target,), device_id_type=MESH
    )
    copy.start()
    return copy


def wrap(value, n):
    return jnp.where(value >= n, value - n, value)


def kernel(
    a_hbm, g_hbm, w_hbm,
    d_hbm, result_hbm,
    d_ref, result, a_in, g_in, w_in,
    at_send, at_recv, g_send, g_recv, at_all, g_all,
    prod0, prod1, prod2, prod3, pair, pair_in, first_in, first_in_p, second_in, second_in_p,
    zsend0, zrecv0, zsend1, zrecv1, plane_sum, ring_sum,
    in_sem, core_s, core_r, pair_s, pair_r, first_s, first_r, second_s, second_r,
    z0_s, z0_r, z1_s, z1_r, p_s, p_r, q_s, q_r, d_sem, result_sem,
    order, near1, near2, near4, near_twin,
):
    me = lax.axis_index("dp")
    core = lax.rem(me, 2)
    x = lax.rem(me // 2, NX)
    y = lax.rem(me // (2 * NX), NY)
    z = me // PLANE
    q = lax.rem(me, PLANE)
    parity = lax.rem(z, 2)

    def device(z_, y_, x_, c_):
        return ((z_ * NY + y_) * NX + x_) * 2 + c_

    loads = []
    for i, (src, dst) in enumerate(((a_hbm, a_in), (g_hbm, g_in), (w_hbm, w_in))):
        copy = pltpu.make_async_copy(src, dst, in_sem.at[i])
        copy.start()
        loads.append(copy)

    def up(k):
        return device(wrap(z + k, NZ), y, x, core)

    def signal(semaphore, *targets):
        for target in targets:
            pl.semaphore_signal(
                semaphore, inc=1, device_id=(target,), device_id_type=MESH
            )

    twin = device(z, y, x, 1 - core)
    signal(
        pltpu.get_barrier_semaphore(), up(1), up(NZ - 1),
        *[device(z, y, wrap(x + k, NX), core) for k in HOPS],
        *[device(z, wrap(y + k, NY), x, core) for k in HOPS],
        twin,
    )

    row = lax.broadcasted_iota(jnp.int32, (512, 512), 0)
    column = lax.broadcasted_iota(jnp.int32, (512, 512), 1)
    wanted = (
        ((row >> 2) & 3) * 128
        + ((row >> 4) & 1) * 64
        + ((row >> 5) & 3) * 16
        + ((row >> 7) & 3) * 4
        + (row & 3)
    )
    order[...] = jnp.where(wanted == column, 1.0, 0.0).astype(jnp.bfloat16)

    def rows_of(c_):
        half = a_in[:, pl.ds(pl.multiple_of(c_ * 512, 512), 512)]
        return lax.dot_general(
            order[...], half, (((1,), (1,)), ((), ())), preferred_element_type=jnp.float32
        )

    loads[0].wait()
    at_send[...] = rows_of(1 - core)
    loads[1].wait()
    for u in range(4):
        piece = g_in[:, STARTS[u] : STARTS[u] + 256]
        g_send[u] = piece.astype(jnp.float32)

    pl.semaphore_wait(pltpu.get_barrier_semaphore(), 9)

    across = {4: push(at_send, at_recv, core_s.at[4], core_r.at[4], twin)}
    for u in (*PLAIN, *PAIRED):
        across[u] = push(g_send.at[u], g_recv.at[u], core_s.at[u], core_r.at[u], twin)
    signal(near1, up(1), up(NZ - 1))

    at_all[:, :, :, :, 0:TOK] = rows_of(core).astype(jnp.bfloat16).reshape(4, 4, 2, 16, TOK)
    for u in range(4):
        g_all[u, 0:TOK, :] = g_in[:, STARTS[u] : STARTS[u] + 256]
    across[4].wait_recv()
    at_all[:, :, :, :, TOK : 2 * TOK] = (
        at_recv[...].astype(jnp.bfloat16).reshape(4, 4, 2, 16, TOK)
    )

    def times(rows, u):
        return jnp.dot(rows, g_all[u], preferred_element_type=jnp.float32)

    def block(u, k):
        rows = at_all[k] if u % 2 == 0 else at_all[:, k]
        return times(rows.reshape(128, 2 * TOK), u).reshape(4, 32, WIDTHS[u])

    def block_of(u, k, parity_):
        rows = at_all[k, :, parity_] if u % 2 == 0 else at_all[:, k, parity_]
        return times(rows.reshape(64, 2 * TOK), u).reshape(4, 16, WIDTHS[u])

    def places(u):
        return (x, y) if u % 2 == 0 else (y, x)

    def along(u, stage, k):
        if (u % 2 == 0) == (stage == 0):
            return device(z, y, k, core)
        return device(z, k, x, core)

    prod = (prod0, prod1, prod2, prod3)
    odd = parity == 1
    mates = {
        2: jnp.where(odd, up(NZ - 1), up(1)),
        3: jnp.where(odd, up(1), up(NZ - 1)),
    }
    sent_pair, sent_first, sent_second = {}, {}, {}

    def send_first(u, hop):
        k = wrap(places(u)[0] + hop, 4)
        into = first_in if u in PLAIN else first_in_p
        sent_first[u, hop] = push(
            prod[u].at[hop], into.at[u % 2, hop - 1],
            first_s.at[u, hop - 1], first_r.at[u, hop - 1], along(u, 0, k),
        )

    def start_plain(u, hop):
        prod[u][hop] = block(u, wrap(places(u)[0] + hop, 4))
        send_first(u, hop)

    def start_paired(u, hop):
        pair[u - 2, hop] = block_of(u, wrap(places(u)[0] + hop, 4), 1 - parity)
        sent_pair[u, hop] = push(
            pair.at[u - 2, hop], pair_in.at[u - 2, hop],
            pair_s.at[u - 2, hop], pair_r.at[u - 2, hop], mates[u],
        )

    for hop in (*HOPS, 0):
        for u in range(4):
            if hop == HOPS[0]:
                across[u].wait_recv()
                g_all[u, TOK : 2 * TOK, :] = g_recv[u].astype(jnp.bfloat16)
            if u in PAIRED:
                start_paired(u, hop)
            elif hop:
                start_plain(u, hop)
    for hop in (*HOPS, 0):
        for u in PAIRED:
            prod[u][hop] = block_of(u, wrap(places(u)[0] + hop, 4), parity)
    for u in PLAIN:
        prod[u][0] = block(u, places(u)[0])

    def cotangent(h):
        d_ref[:, h * 256 : (h + 1) * 256] = lax.dot_general(
            g_in[...], w_in[h * 256 : (h + 1) * 256, :], (((1,), (1,)), ((), ())),
            preferred_element_type=jnp.float32,
        ).astype(jnp.bfloat16)

    for hop in HOPS:
        for u in PAIRED:
            sent_pair[u, hop].wait_recv()
            prod[u][hop] = prod[u][hop] + pair_in[u - 2, hop]
            send_first(u, hop)

    pl.semaphore_wait(near1, 2)
    signal(near2, up(2), up(NZ - 2))
    loads[2].wait()
    for h in range(4):
        cotangent(h)
    d_store = pltpu.make_async_copy(d_ref, d_hbm, d_sem)
    d_store.start()
    pl.semaphore_wait(near2, 2)
    signal(near4, up(4), up(NZ - 4))

    def end_first(u):
        into = first_in if u in PLAIN else first_in_p
        if u in PAIRED:
            sent_pair[u, 0].wait_recv()
        for hop in (1, 3, 2):
            sent_first[u, hop].wait_recv()
        i = u % 2
        total = prod[u][0] + into[i, 0] + into[i, 1] + into[i, 2]
        if u in PAIRED:
            total = total + pair_in[u - 2, 0]
        prod[u][0] = total
        into = second_in if u in PLAIN else second_in_p
        for hop in HOPS:
            k = wrap(places(u)[1] + hop, 4)
            sent_second[u, hop] = push(
                prod[u].at[0, k], into.at[i, hop - 1],
                second_s.at[u, hop - 1], second_r.at[u, hop - 1], along(u, 1, k),
            )

    def end_second(u, zsend):
        into = second_in if u in PLAIN else second_in_p
        for hop in (1, 3, 2):
            sent_second[u, hop].wait_recv()
        i = u % 2
        total = prod[u][0, places(u)[1]] + into[i, 0] + into[i, 1] + into[i, 2]
        start = STARTS[u] - STARTS[u - i]
        for k in range(zsend.shape[0]):
            to = k if u in PAIRED else (k % 8 // 2 * 2 + k // 8) * 2 + k % 2
            zsend[to, :, start : start + WIDTHS[u]] = total[2 * k : 2 * k + 2]

    def along_z(zsend, zrecv, s, r, slot, near, count, z_of):
        for offset in sorted(range(count), key=lambda k: -min(k, count - k)):
            place = wrap(near + offset, count)
            z_ = z_of(place)
            for c_ in (core, 1 - core):
                k = place * 2 + c_
                if offset == 0 and c_ is core:
                    mine = z_ == z

                    @pl.when(jnp.logical_not(mine))
                    def _():
                        push(zsend.at[k], zrecv.at[slot], s, r, device(z_, y, x, c_))

                    @pl.when(mine)
                    def _():
                        pltpu.make_async_copy(zsend.at[k], zrecv.at[slot], r).start()
                else:
                    push(zsend.at[k], zrecv.at[slot], s, r, device(z_, y, x, c_))

    for u in PLAIN:
        end_first(u)
    pl.semaphore_wait(near4, 2)
    signal(near_twin, twin)
    for u in PAIRED:
        end_first(u)
    for u in PLAIN:
        end_second(u, zsend0)
    pl.semaphore_wait(near_twin, 1)
    along_z(
        zsend0, zrecv0, z0_s, z0_r, z, lax.rem(z, 8), 8, lambda place: 8 * core + place
    )
    for u in PAIRED:
        end_second(u, zsend1)
    along_z(
        zsend1, zrecv1, z1_s, z1_r, z // 2, lax.rem(z // 2, 4), 4,
        lambda place: 8 * core + 2 * place + parity,
    )

    def gather_z(zrecv, r):
        pltpu.make_async_copy(zrecv, zrecv, r).wait()
        total = zrecv[0]
        for k in range(1, zrecv.shape[0]):
            total = total + zrecv[k]
        return total

    plain = gather_z(zrecv0, z0_r)
    result[0:2, 0:WIDE0] = plain
    paired = gather_z(zrecv1, z1_r)
    result[0:2, WIDE0:1024] = paired

    def spread(slots, slot, count, first, wrapped, target, s, r, value):
        slots[slot] = value

        def start(k, _):
            push(slots.at[slot], slots.at[slot], s, r, target(wrapped(k)))
            return 0

        lax.fori_loop(first, first + count - 1, start, 0)
        arrived = slots.at[pl.ds(0, count - 1)]
        pltpu.make_async_copy(arrived, arrived, r).wait()
        return jnp.sum(slots[...], axis=0)

    square = jnp.zeros((1, 128), jnp.float32)
    for part in (plain, paired):
        lanes = jnp.sum(part * part, axis=0, keepdims=True)
        for k in range(part.shape[1] // 128):
            square = square + lanes[:, k * 128 : (k + 1) * 128]
    base = z * PLANE
    square = spread(
        plane_sum, q, PLANE, 1, lambda k: wrap(q + k, PLANE), lambda k: base + k, p_s, p_r, square
    )
    result[2:3, 0:128] = spread(
        ring_sum, z, NZ, 8, lambda k: wrap(wrap(z + k + jnp.where(k >= NZ, 1, 0), NZ), NZ),
        lambda k: k * PLANE + q, q_s, q_r, square,
    )

    store = pltpu.make_async_copy(result, result_hbm, result_sem)
    store.start()
    store.wait()
    d_store.wait()
    for sent in (across, sent_pair, sent_first, sent_second):
        for copy in sent.values():
            copy.wait_send()

    def left(buffer, count, s):
        gone = buffer.at[pl.ds(0, count)]
        pltpu.make_async_copy(gone, gone, s).wait()

    at_home = (z // 8) == core

    @pl.when(at_home)
    def _():
        left(zsend0, 15, z0_s)
        left(zsend1, 7, z1_s)

    @pl.when(jnp.logical_not(at_home))
    def _():
        left(zsend0, 16, z0_s)
        left(zsend1, 8, z1_s)

    left(plane_sum, PLANE - 1, p_s)
    left(ring_sum, NZ - 1, q_s)


def update_kernel(
    d_hbm, result_hbm, cm_hbm, cv_hbm, ma_hbm, sm_hbm, sv_hbm,
    d_out, mu_out, vu_out, nm_out,
    result, cm, cv, ma, sm, sv, mu, vu, nm, d, load_sem, store_sem,
):
    stores = [
        pltpu.make_async_copy(src, dst, store_sem.at[i])
        for i, (src, dst) in enumerate(((d, d_out), (mu, mu_out), (vu, vu_out), (nm, nm_out)))
    ]
    loads = [
        pltpu.make_async_copy(src, dst, load_sem.at[i])
        for i, (src, dst) in enumerate(
            (
                (result_hbm, result), (cm_hbm, cm), (cv_hbm, cv), (ma_hbm, ma),
                (sm_hbm, sm), (sv_hbm, sv), (d_hbm, d),
            )
        )
    ]
    for load in loads:
        load.start()
    for load in loads[:-1]:
        load.wait()
    squares = jnp.sum(result[2:3, 0:128], axis=1, keepdims=True)
    clip = jnp.minimum(1.0, 1.0 / jnp.sqrt(squares + 1e-12))
    scale_m, scale_v = sm[0], sv[0]
    for p in range(2):
        part = slice(p * 1024, (p + 1) * 1024)
        m_old = scale_m * (cm[:, part].astype(jnp.float32) - 127.0) / 127.0
        ratio_v = cv[:, part].astype(jnp.float32) / 255.0
        v_old = scale_v * ratio_v * ratio_v
        clipped = clip * result[p : p + 1, :]
        m_new = 0.9 * m_old + 0.1 * clipped
        v_new = 0.95 * v_old + 0.05 * clipped * clipped
        update = m_new / (1.0 - 0.9**STEP) / (jnp.sqrt(v_new / (1.0 - 0.95**STEP)) + 1e-08)
        nm[:, part] = ma[:, part] - 0.01 * (update + 0.1 * ma[:, part])
        mu[:, part] = m_new / scale_m
        vu[:, part] = v_new / scale_v
    for store in stores[1:]:
        store.start()
    loads[-1].wait()
    stores[0].start()
    for store in stores:
        store.wait()


def local(attn_out, grad_out, w_out, codes_m, codes_v, scale_m, scale_v, master):
    f32, bf16 = jnp.float32, jnp.bfloat16
    vmem, dma = pltpu.VMEM, pltpu.SemaphoreType.DMA
    shape = jax.ShapeDtypeStruct
    hbm = pl.BlockSpec(memory_space=pltpu.HBM)
    block = shape((1, 2048), f32)
    d_attn, result = pl.pallas_call(
        kernel,
        out_shape=(shape((TOK, 1024), bf16), shape((4, 1024), f32)),
        in_specs=[hbm] * 3,
        out_specs=(hbm,) * 2,
        scratch_shapes=[
            vmem((TOK, 1024), bf16),
            vmem((4, 1024), f32),
            vmem((TOK, 1024), bf16),
            vmem((TOK, 1024), bf16),
            vmem((1024, 1024), bf16),
            vmem((512, TOK), f32),
            vmem((512, TOK), f32),
            vmem((4, TOK, 256), f32),
            vmem((4, TOK, 256), f32),
            vmem((4, 4, 2, 16, 2 * TOK), bf16),
            vmem((4, 2 * TOK, 256), bf16),
            vmem((4, 4, 32, WIDTHS[0]), f32),
            vmem((4, 4, 32, WIDTHS[1]), f32),
            vmem((4, 4, 16, WIDTHS[2]), f32),
            vmem((4, 4, 16, WIDTHS[3]), f32),
            vmem((2, 4, 4, 16, WIDTHS[2]), f32),
            vmem((2, 4, 4, 16, WIDTHS[2]), f32),
            vmem((2, 3, 4, 32, WIDTHS[0]), f32),
            vmem((2, 3, 4, 16, WIDTHS[2]), f32),
            vmem((2, 3, 32, WIDTHS[0]), f32),
            vmem((2, 3, 16, WIDTHS[2]), f32),
            vmem((16, 2, WIDE0), f32),
            vmem((16, 2, WIDE0), f32),
            vmem((8, 2, WIDE1), f32),
            vmem((8, 2, WIDE1), f32),
            vmem((PLANE, 1, 128), f32),
            vmem((NZ, 1, 128), f32),
            dma((3,)),
            dma((5,)),
            dma((5,)),
            dma((2, 4)),
            dma((2, 4)),
            dma((4, 3)),
            dma((4, 3)),
            dma((4, 3)),
            dma((4, 3)),
            *[dma] * 10,
            vmem((512, 512), bf16),
            *[pltpu.SemaphoreType.REGULAR] * 4,
        ],
        compiler_params=pltpu.CompilerParams(
            collective_id=0, has_side_effects=True, vmem_limit_bytes=60 * 2**20
        ),
        cost_estimate=pl.CostEstimate(
            flops=2 * 2 * TOK * 1024 * 1024, bytes_accessed=3 * 2**20, transcendentals=0
        ),
    )(attn_out, grad_out, w_out)
    return pl.pallas_call(
        update_kernel,
        out_shape=(shape((TOK, 1024), bf16), block, block, block),
        in_specs=[hbm] * 7,
        out_specs=(hbm,) * 4,
        scratch_shapes=[
            vmem((4, 1024), f32),
            vmem((1, 2048), jnp.int32),
            vmem((1, 2048), jnp.int32),
            vmem((1, 2048), f32),
            pltpu.SMEM((1,), f32),
            pltpu.SMEM((1,), f32),
            vmem((1, 2048), f32),
            vmem((1, 2048), f32),
            vmem((1, 2048), f32),
            vmem((TOK, 1024), bf16),
            dma((7,)),
            dma((4,)),
        ],
        compiler_params=pltpu.CompilerParams(vmem_limit_bytes=60 * 2**20),
        cost_estimate=pl.CostEstimate(flops=2048 * 30, bytes_accessed=2**19, transcendentals=4096),
    )(d_attn, result, codes_m, codes_v, master, scale_m, scale_v)


def solution(mesh):
    in_specs = (
        P("dp", None),
        P("dp", None),
        P(),
        P("dp", None),
        P("dp", None),
        P("dp"),
        P("dp"),
        P("dp", None),
    )
    out_specs = (P("dp", None), P("dp", None), P("dp", None), P("dp", None))
    return jax.shard_map(local, mesh=mesh, in_specs=in_specs, out_specs=out_specs, check_vma=False)
```

```python
import functools

import jax
import jax.numpy as jnp
from jax import lax
from jax.experimental import pallas as pl
from jax.experimental.pallas import tpu as pltpu
from jax.sharding import PartitionSpec as P

STEP = 100
NX, NY, NZ = 4, 4, 16
PLANE = NX * NY * 2
TOK = 128
WIDTHS = (256, 256, 256, 256)
STARTS = tuple(sum(WIDTHS[:u]) for u in range(4))
PLAIN, PAIRED = (0, 1), (2, 3)
WIDE0, WIDE1 = WIDTHS[0] + WIDTHS[1], WIDTHS[2] + WIDTHS[3]
HOPS = (2, 1, 3)
MESH = pl.DeviceIdType.MESH


def push(src, dst, s, r, target):
    copy = pltpu.make_async_remote_copy(
        src_ref=src, dst_ref=dst, send_sem=s, recv_sem=r, device_id=(target,), device_id_type=MESH
    )
    copy.start()
    return copy


def wrap(value, n):
    return jnp.where(value >= n, value - n, value)


def kernel(
    a_hbm, g_hbm, w_hbm,
    d_hbm, result_hbm,
    d_ref, result, a_in, g_in, w_in,
    at_send, at_recv, at_all,
    gs0, gs1, gs2, gs3, gr0, gr1, gr2, gr3, ga0, ga1, ga2, ga3,
    prod0, prod1, prod2, prod3, pair, pair_in, first_in, first_in_p, second_in, second_in_p,
    zsend0, zrecv0, zsend1, zrecv1, plane_sum, ring_sum,
    in_sem, core_s, core_r, pair_s, pair_r, first_s, first_r, second_s, second_r,
    z0_s, z0_r, z1_s, z1_r, p_s, p_r, q_s, q_r, d_sem, result_sem,
    order, near1, near2, near4, near_twin,
):
    me = lax.axis_index("dp")
    core = lax.rem(me, 2)
    x = lax.rem(me // 2, NX)
    y = lax.rem(me // (2 * NX), NY)
    z = me // PLANE
    q = lax.rem(me, PLANE)
    parity = lax.rem(z, 2)

    def device(z_, y_, x_, c_):
        return ((z_ * NY + y_) * NX + x_) * 2 + c_

    loads = []
    for i, (src, dst) in enumerate(((g_hbm, g_in), (a_hbm, a_in), (w_hbm, w_in))):
        copy = pltpu.make_async_copy(src, dst, in_sem.at[i])
        copy.start()
        loads.append(copy)

    def up(k):
        return device(wrap(z + k, NZ), y, x, core)

    def signal(semaphore, *targets):
        for target in targets:
            pl.semaphore_signal(
                semaphore, inc=1, device_id=(target,), device_id_type=MESH
            )

    twin = device(z, y, x, 1 - core)
    signal(
        pltpu.get_barrier_semaphore(), up(1), up(NZ - 1),
        *[device(z, y, wrap(x + k, NX), core) for k in HOPS],
        *[device(z, wrap(y + k, NY), x, core) for k in HOPS],
        twin,
    )

    row = lax.broadcasted_iota(jnp.int32, (512, 512), 0)
    column = lax.broadcasted_iota(jnp.int32, (512, 512), 1)
    wanted = (
        ((row >> 2) & 3) * 128
        + ((row >> 4) & 1) * 64
        + ((row >> 5) & 3) * 16
        + ((row >> 7) & 3) * 4
        + (row & 3)
    )
    order[...] = jnp.where(wanted == column, 1.0, 0.0).astype(jnp.bfloat16)

    def rows_of(c_):
        half = a_in[:, pl.ds(pl.multiple_of(c_ * 512, 512), 512)]
        return lax.dot_general(
            order[...], half, (((1,), (1,)), ((), ())), preferred_element_type=jnp.float32
        )

    g_send, g_recv, g_all = (gs0, gs1, gs2, gs3), (gr0, gr1, gr2, gr3), (ga0, ga1, ga2, ga3)
    across = {}

    def cross(u):
        piece = g_in[:, STARTS[u] : STARTS[u] + WIDTHS[u]]
        g_send[u][...] = piece.astype(jnp.float32)
        if u == 0:
            pl.semaphore_wait(pltpu.get_barrier_semaphore(), 9)
        across[u] = push(g_send[u], g_recv[u], core_s.at[u], core_r.at[u], twin)
        g_all[u][0:TOK, :] = piece

    loads[0].wait()
    for u in PLAIN:
        cross(u)
    loads[1].wait()
    at_send[...] = rows_of(1 - core)
    across[4] = push(at_send, at_recv, core_s.at[4], core_r.at[4], twin)
    for u in PAIRED:
        cross(u)
    signal(near1, up(1), up(NZ - 1))

    at_all[:, :, :, :, 0:TOK] = rows_of(core).astype(jnp.bfloat16).reshape(4, 4, 2, 16, TOK)
    across[4].wait_recv()
    at_all[:, :, :, :, TOK : 2 * TOK] = (
        at_recv[...].astype(jnp.bfloat16).reshape(4, 4, 2, 16, TOK)
    )

    def times(rows, u):
        return jnp.dot(rows, g_all[u][...], preferred_element_type=jnp.float32)

    def block(u, k):
        rows = at_all[k] if u % 2 == 0 else at_all[:, k]
        return times(rows.reshape(128, 2 * TOK), u).reshape(4, 32, WIDTHS[u])

    def block_of(u, k, parity_):
        rows = at_all[k, :, parity_] if u % 2 == 0 else at_all[:, k, parity_]
        return times(rows.reshape(64, 2 * TOK), u).reshape(4, 16, WIDTHS[u])

    def places(u):
        return (x, y) if u % 2 == 0 else (y, x)

    def along(u, stage, k):
        if (u % 2 == 0) == (stage == 0):
            return device(z, y, k, core)
        return device(z, k, x, core)

    prod = (prod0, prod1, prod2, prod3)
    odd = parity == 1
    mates = {
        2: jnp.where(odd, up(NZ - 1), up(1)),
        3: jnp.where(odd, up(1), up(NZ - 1)),
    }
    sent_pair, sent_first, sent_second = {}, {}, {}

    def send_first(u, hop):
        k = wrap(places(u)[0] + hop, 4)
        into = first_in if u in PLAIN else first_in_p
        sent_first[u, hop] = push(
            prod[u].at[hop], into.at[u % 2, hop - 1],
            first_s.at[u, hop - 1], first_r.at[u, hop - 1], along(u, 0, k),
        )

    def start_plain(u, hop):
        prod[u][hop] = block(u, wrap(places(u)[0] + hop, 4))
        send_first(u, hop)

    def start_paired(u, hop):
        pair[u - 2, hop] = block_of(u, wrap(places(u)[0] + hop, 4), 1 - parity)
        sent_pair[u, hop] = push(
            pair.at[u - 2, hop], pair_in.at[u - 2, hop],
            pair_s.at[u - 2, hop], pair_r.at[u - 2, hop], mates[u],
        )

    for hop in (*HOPS, 0):
        for u in range(4):
            if hop == HOPS[0]:
                across[u].wait_recv()
                g_all[u][TOK : 2 * TOK, :] = g_recv[u][...].astype(jnp.bfloat16)
            if u in PAIRED:
                start_paired(u, hop)
            elif hop:
                start_plain(u, hop)
        if hop == HOPS[0]:
            pl.semaphore_wait(near1, 2)
            signal(near2, up(2), up(NZ - 2))
    for hop in (*HOPS, 0):
        for u in PAIRED:
            prod[u][hop] = block_of(u, wrap(places(u)[0] + hop, 4), parity)
    for u in PLAIN:
        prod[u][0] = block(u, places(u)[0])

    def cotangent(h):
        d_ref[:, h * 256 : (h + 1) * 256] = lax.dot_general(
            g_in[...], w_in[h * 256 : (h + 1) * 256, :], (((1,), (1,)), ((), ())),
            preferred_element_type=jnp.float32,
        ).astype(jnp.bfloat16)

    pl.semaphore_wait(near2, 2)
    signal(near4, up(4), up(NZ - 4))
    for hop in HOPS:
        for u in PAIRED:
            sent_pair[u, hop].wait_recv()
            prod[u][hop] = prod[u][hop] + pair_in[u - 2, hop]
            send_first(u, hop)

    loads[2].wait()
    for h in range(4):
        cotangent(h)
    d_store = pltpu.make_async_copy(d_ref, d_hbm, d_sem)
    d_store.start()
    pl.semaphore_wait(near4, 2)
    signal(near_twin, twin)

    def end_first(u):
        into = first_in if u in PLAIN else first_in_p
        if u in PAIRED:
            sent_pair[u, 0].wait_recv()
        for hop in (1, 3, 2):
            sent_first[u, hop].wait_recv()
        i = u % 2
        total = prod[u][0] + into[i, 0] + into[i, 1] + into[i, 2]
        if u in PAIRED:
            total = total + pair_in[u - 2, 0]
        prod[u][0] = total
        into = second_in if u in PLAIN else second_in_p
        for hop in HOPS:
            k = wrap(places(u)[1] + hop, 4)
            sent_second[u, hop] = push(
                prod[u].at[0, k], into.at[i, hop - 1],
                second_s.at[u, hop - 1], second_r.at[u, hop - 1], along(u, 1, k),
            )

    def end_second(u, zsend):
        into = second_in if u in PLAIN else second_in_p
        for hop in (1, 3, 2):
            sent_second[u, hop].wait_recv()
        i = u % 2
        total = prod[u][0, places(u)[1]] + into[i, 0] + into[i, 1] + into[i, 2]
        start = STARTS[u] - STARTS[u - i]
        for k in range(zsend.shape[0]):
            to = k if u in PAIRED else (k % 8 // 2 * 2 + k // 8) * 2 + k % 2
            zsend[to, :, start : start + WIDTHS[u]] = total[2 * k : 2 * k + 2]

    def along_z(zsend, zrecv, s, r, slot, near, count, z_of):
        for offset in sorted(range(count), key=lambda k: -min(k, count - k)):
            place = wrap(near + offset, count)
            z_ = z_of(place)
            for c_ in (core, 1 - core):
                k = place * 2 + c_
                if offset == 0 and c_ is core:
                    mine = z_ == z

                    @pl.when(jnp.logical_not(mine))
                    def _():
                        push(zsend.at[k], zrecv.at[slot], s, r, device(z_, y, x, c_))

                    @pl.when(mine)
                    def _():
                        pltpu.make_async_copy(zsend.at[k], zrecv.at[slot], r).start()
                else:
                    push(zsend.at[k], zrecv.at[slot], s, r, device(z_, y, x, c_))

    for u in PLAIN:
        end_first(u)
    for u in PAIRED:
        end_first(u)
    for u in PLAIN:
        end_second(u, zsend0)
    pl.semaphore_wait(near_twin, 1)
    along_z(
        zsend0, zrecv0, z0_s, z0_r, z, lax.rem(z, 8), 8, lambda place: 8 * core + place
    )
    for u in PAIRED:
        end_second(u, zsend1)
    along_z(
        zsend1, zrecv1, z1_s, z1_r, z // 2, lax.rem(z // 2, 4), 4,
        lambda place: 8 * core + 2 * place + parity,
    )

    def gather_z(zrecv, r):
        pltpu.make_async_copy(zrecv, zrecv, r).wait()
        total = zrecv[0]
        for k in range(1, zrecv.shape[0]):
            total = total + zrecv[k]
        return total

    def spill(part, tile):
        for p in range(2):
            for k in range(part.shape[1] // 128):
                at = p * 8 + tile + k
                result[at : at + 1, :] = part[p : p + 1, k * 128 : (k + 1) * 128]

    plain = gather_z(zrecv0, z0_r)
    spill(plain, 0)
    paired = gather_z(zrecv1, z1_r)
    spill(paired, WIDE0 // 128)

    def spread(slots, slot, targets, s, r, value):
        slots[slot] = value
        for target in targets:
            push(slots.at[slot], slots.at[slot], s, r, target)
        arrived = slots.at[pl.ds(0, len(targets))]
        pltpu.make_async_copy(arrived, arrived, r).wait()
        return jnp.sum(slots[...], axis=0)

    square = jnp.zeros((1, 128), jnp.float32)
    for part in (plain, paired):
        lanes = jnp.sum(part * part, axis=0, keepdims=True)
        for k in range(part.shape[1] // 128):
            square = square + lanes[:, k * 128 : (k + 1) * 128]
    away = [(j, i) for j in range(NY) for i in range(NX)]
    away.sort(key=lambda k: -min(k[0], NY - k[0]) - min(k[1], NX - k[1]))
    plane = [
        device(z, wrap(y + j, NY), wrap(x + i, NX), c_)
        for j, i in away for c_ in (1 - core, core) if j or i
    ]
    square = spread(plane_sum, q, plane + [twin], p_s, p_r, square)
    ring = sorted(range(1, NZ), key=lambda k: -min(k, NZ - k))
    result[16:17, :] = spread(ring_sum, z, [up(k) for k in ring], q_s, q_r, square)

    store = pltpu.make_async_copy(result, result_hbm, result_sem)
    store.start()
    store.wait()
    d_store.wait()
    for sent in (across, sent_pair, sent_first, sent_second):
        for copy in sent.values():
            copy.wait_send()

    def left(buffer, count, s):
        gone = buffer.at[pl.ds(0, count)]
        pltpu.make_async_copy(gone, gone, s).wait()

    at_home = (z // 8) == core

    @pl.when(at_home)
    def _():
        left(zsend0, 15, z0_s)
        left(zsend1, 7, z1_s)

    @pl.when(jnp.logical_not(at_home))
    def _():
        left(zsend0, 16, z0_s)
        left(zsend1, 8, z1_s)

    left(plane_sum, PLANE - 1, p_s)
    left(ring_sum, NZ - 1, q_s)


def update_kernel(
    d_hbm, result_hbm, cm_hbm, cv_hbm, ma_hbm, sm_hbm, sv_hbm,
    d_out, mu_out, vu_out, nm_out,
    result, cm, cv, ma, sm, sv, mu, vu, nm, d, load_sem, store_sem,
):
    stores = [
        pltpu.make_async_copy(src, dst, store_sem.at[i])
        for i, (src, dst) in enumerate(((d, d_out), (mu, mu_out), (vu, vu_out), (nm, nm_out)))
    ]
    loads = [
        pltpu.make_async_copy(src, dst, load_sem.at[i])
        for i, (src, dst) in enumerate(
            (
                (result_hbm, result), (cm_hbm, cm), (cv_hbm, cv), (ma_hbm, ma),
                (sm_hbm, sm), (sv_hbm, sv), (d_hbm, d),
            )
        )
    ]
    for load in loads:
        load.start()
    for load in loads[:-1]:
        load.wait()
    squares = jnp.sum(result[16:17, :], axis=1, keepdims=True)
    clip = jnp.minimum(1.0, 1.0 / jnp.sqrt(squares + 1e-12))
    scale_m, scale_v = sm[0], sv[0]
    m_old = scale_m * (cm[...].astype(jnp.float32) - 127.0) / 127.0
    ratio_v = cv[...].astype(jnp.float32) / 255.0
    v_old = scale_v * ratio_v * ratio_v
    clipped = clip * result[0:16, :]
    m_new = 0.9 * m_old + 0.1 * clipped
    v_new = 0.95 * v_old + 0.05 * clipped * clipped
    update = m_new / (1.0 - 0.9**STEP) / (jnp.sqrt(v_new / (1.0 - 0.95**STEP)) + 1e-08)
    nm[...] = ma[...] - 0.01 * (update + 0.1 * ma[...])
    mu[...] = m_new / scale_m
    vu[...] = v_new / scale_v
    for store in stores[1:]:
        store.start()
    loads[-1].wait()
    stores[0].start()
    for store in stores:
        store.wait()


def local(attn_out, grad_out, w_out, codes_m, codes_v, scale_m, scale_v, master):
    f32, bf16 = jnp.float32, jnp.bfloat16
    vmem, dma = pltpu.VMEM, pltpu.SemaphoreType.DMA
    shape = jax.ShapeDtypeStruct
    hbm = pl.BlockSpec(memory_space=pltpu.HBM)
    block = shape((16, 128), f32)
    d_attn, result = pl.pallas_call(
        kernel,
        out_shape=(shape((TOK, 1024), bf16), shape((24, 128), f32)),
        in_specs=[hbm] * 3,
        out_specs=(hbm,) * 2,
        scratch_shapes=[
            vmem((TOK, 1024), bf16),
            vmem((24, 128), f32),
            vmem((TOK, 1024), bf16),
            vmem((TOK, 1024), bf16),
            vmem((1024, 1024), bf16),
            vmem((512, TOK), f32),
            vmem((512, TOK), f32),
            vmem((4, 4, 2, 16, 2 * TOK), bf16),
            *[vmem((TOK, w), f32) for w in WIDTHS],
            *[vmem((TOK, w), f32) for w in WIDTHS],
            *[vmem((2 * TOK, w), bf16) for w in WIDTHS],
            vmem((4, 4, 32, WIDTHS[0]), f32),
            vmem((4, 4, 32, WIDTHS[1]), f32),
            vmem((4, 4, 16, WIDTHS[2]), f32),
            vmem((4, 4, 16, WIDTHS[3]), f32),
            vmem((2, 4, 4, 16, WIDTHS[2]), f32),
            vmem((2, 4, 4, 16, WIDTHS[2]), f32),
            vmem((2, 3, 4, 32, WIDTHS[0]), f32),
            vmem((2, 3, 4, 16, WIDTHS[2]), f32),
            vmem((2, 3, 32, WIDTHS[0]), f32),
            vmem((2, 3, 16, WIDTHS[2]), f32),
            vmem((16, 2, WIDE0), f32),
            vmem((16, 2, WIDE0), f32),
            vmem((8, 2, WIDE1), f32),
            vmem((8, 2, WIDE1), f32),
            vmem((PLANE, 1, 128), f32),
            vmem((NZ, 1, 128), f32),
            dma((3,)),
            dma((5,)),
            dma((5,)),
            dma((2, 4)),
            dma((2, 4)),
            dma((4, 3)),
            dma((4, 3)),
            dma((4, 3)),
            dma((4, 3)),
            *[dma] * 10,
            vmem((512, 512), bf16),
            *[pltpu.SemaphoreType.REGULAR] * 4,
        ],
        compiler_params=pltpu.CompilerParams(
            collective_id=0, has_side_effects=True, vmem_limit_bytes=60 * 2**20
        ),
        cost_estimate=pl.CostEstimate(
            flops=2 * 2 * TOK * 1024 * 1024, bytes_accessed=3 * 2**20, transcendentals=0
        ),
    )(attn_out, grad_out, w_out)
    d_attn, m_unit, v_unit, new_master = pl.pallas_call(
        update_kernel,
        out_shape=(shape((TOK, 1024), bf16), block, block, block),
        in_specs=[hbm] * 7,
        out_specs=(hbm,) * 4,
        scratch_shapes=[
            vmem((24, 128), f32),
            vmem((16, 128), jnp.int32),
            vmem((16, 128), jnp.int32),
            vmem((16, 128), f32),
            pltpu.SMEM((1,), f32),
            pltpu.SMEM((1,), f32),
            vmem((16, 128), f32),
            vmem((16, 128), f32),
            vmem((16, 128), f32),
            vmem((TOK, 1024), bf16),
            dma((7,)),
            dma((4,)),
        ],
        compiler_params=pltpu.CompilerParams(vmem_limit_bytes=60 * 2**20),
        cost_estimate=pl.CostEstimate(flops=2048 * 30, bytes_accessed=2**19, transcendentals=4096),
    )(
        d_attn, result, codes_m.reshape(16, 128), codes_v.reshape(16, 128),
        master.reshape(16, 128), scale_m, scale_v,
    )
    return (
        d_attn, m_unit.reshape(1, 2048), v_unit.reshape(1, 2048), new_master.reshape(1, 2048)
    )


def solution(mesh):
    in_specs = (
        P("dp", None),
        P("dp", None),
        P(),
        P("dp", None),
        P("dp", None),
        P("dp"),
        P("dp"),
        P("dp", None),
    )
    out_specs = (P("dp", None), P("dp", None), P("dp", None), P("dp", None))
    return jax.shard_map(local, mesh=mesh, in_specs=in_specs, out_specs=out_specs, check_vma=False)
```

```python
import functools

import jax
import jax.numpy as jnp
from jax import lax
from jax.experimental import pallas as pl
from jax.experimental.pallas import tpu as pltpu
from jax.sharding import PartitionSpec as P

STEP = 100
NX, NY, NZ = 4, 4, 16
PLANE = NX * NY * 2
TOK = 128
VMEM = int(53.5 * 2**20)
WIDTHS = (256, 256, 256, 256)
STARTS = tuple(sum(WIDTHS[:u]) for u in range(4))
PLAIN, PAIRED = (0, 1), (2, 3)
WIDE0, WIDE1 = WIDTHS[0] + WIDTHS[1], WIDTHS[2] + WIDTHS[3]
HOPS = (2, 1, 3)
MESH = pl.DeviceIdType.MESH


def push(src, dst, s, r, target):
    copy = pltpu.make_async_remote_copy(
        src_ref=src, dst_ref=dst, send_sem=s, recv_sem=r, device_id=(target,), device_id_type=MESH
    )
    copy.start()
    return copy


def wrap(value, n):
    return jnp.where(value >= n, value - n, value)


def kernel(
    a_hbm, g_hbm, w_hbm,
    d_ref, result,
    a_in, g_in, w_in,
    at_send, at_recv, at_all,
    gs0, gs1, gs2, gs3, gr0, gr1, gr2, gr3, ga0, ga1, ga2, ga3,
    prod0, prod1, prod2, prod3, pair, pair_in, first_in, first_in_p, second_in, second_in_p,
    zsend0, zrecv0, zsend1, zrecv1, plane_sum, ring_sum,
    in_sem, core_s, core_r, pair_s, pair_r, first_s, first_r, second_s, second_r,
    z0_s, z0_r, z1_s, z1_r, p_s, p_r, q_s, q_r,
    order, near1, near2, near4, near_twin,
):
    me = lax.axis_index("dp")
    core = lax.rem(me, 2)
    x = lax.rem(me // 2, NX)
    y = lax.rem(me // (2 * NX), NY)
    z = me // PLANE
    parity = lax.rem(z, 2)

    def device(z_, y_, x_, c_):
        return ((z_ * NY + y_) * NX + x_) * 2 + c_

    loads = []
    for i, (src, dst) in enumerate(((g_hbm, g_in), (a_hbm, a_in), (w_hbm, w_in))):
        copy = pltpu.make_async_copy(src, dst, in_sem.at[i])
        copy.start()
        loads.append(copy)

    def up(k):
        return device(wrap(z + k, NZ), y, x, core)

    def signal(semaphore, *targets):
        for target in targets:
            pl.semaphore_signal(
                semaphore, inc=1, device_id=(target,), device_id_type=MESH
            )

    twin = device(z, y, x, 1 - core)
    signal(
        pltpu.get_barrier_semaphore(), up(1), up(NZ - 1),
        *[device(z, y, wrap(x + k, NX), core) for k in HOPS],
        *[device(z, wrap(y + k, NY), x, core) for k in HOPS],
        twin,
    )

    row = lax.broadcasted_iota(jnp.int32, (512, 512), 0)
    column = lax.broadcasted_iota(jnp.int32, (512, 512), 1)
    wanted = (
        ((row >> 2) & 3) * 128
        + ((row >> 4) & 1) * 64
        + ((row >> 5) & 3) * 16
        + ((row >> 7) & 3) * 4
        + (row & 3)
    )
    order[...] = jnp.where(wanted == column, 1.0, 0.0).astype(jnp.bfloat16)

    def rows_of(c_):
        half = a_in[:, pl.ds(pl.multiple_of(c_ * 512, 512), 512)]
        return lax.dot_general(
            order[...], half, (((1,), (1,)), ((), ())), preferred_element_type=jnp.float32
        )

    g_send, g_recv, g_all = (gs0, gs1, gs2, gs3), (gr0, gr1, gr2, gr3), (ga0, ga1, ga2, ga3)
    across = {}

    def cross(u):
        piece = g_in[:, STARTS[u] : STARTS[u] + WIDTHS[u]]
        g_send[u][...] = piece.astype(jnp.float32)
        if u == 0:
            pl.semaphore_wait(pltpu.get_barrier_semaphore(), 9)
        across[u] = push(g_send[u], g_recv[u], core_s.at[u], core_r.at[u], twin)
        g_all[u][0:TOK, :] = piece

    loads[0].wait()
    cross(0)
    loads[1].wait()
    at_send[...] = rows_of(1 - core)
    across[4] = push(at_send, at_recv, core_s.at[4], core_r.at[4], twin)
    for u in range(1, 4):
        cross(u)
    signal(near1, up(1), up(NZ - 1))

    at_all[:, :, :, :, 0:TOK] = rows_of(core).astype(jnp.bfloat16).reshape(4, 4, 2, 16, TOK)
    across[4].wait_recv()
    at_all[:, :, :, :, TOK : 2 * TOK] = (
        at_recv[...].astype(jnp.bfloat16).reshape(4, 4, 2, 16, TOK)
    )

    def times(rows, u):
        return jnp.dot(rows, g_all[u][...], preferred_element_type=jnp.float32)

    def block(u, k):
        rows = at_all[k] if u % 2 == 0 else at_all[:, k]
        return times(rows.reshape(128, 2 * TOK), u).reshape(4, 32, WIDTHS[u])

    def block_of(u, k, parity_):
        rows = at_all[k, :, parity_] if u % 2 == 0 else at_all[:, k, parity_]
        return times(rows.reshape(64, 2 * TOK), u).reshape(4, 16, WIDTHS[u])

    def places(u):
        return (x, y) if u % 2 == 0 else (y, x)

    def along(u, stage, k):
        if (u % 2 == 0) == (stage == 0):
            return device(z, y, k, core)
        return device(z, k, x, core)

    prod = (prod0, prod1, prod2, prod3)
    odd = parity == 1
    mates = {
        2: jnp.where(odd, up(NZ - 1), up(1)),
        3: jnp.where(odd, up(1), up(NZ - 1)),
    }
    sent_pair, sent_first, sent_second = {}, {}, {}

    def send_first(u, hop):
        k = wrap(places(u)[0] + hop, 4)
        into = first_in if u in PLAIN else first_in_p
        sent_first[u, hop] = push(
            prod[u].at[hop], into.at[u % 2, hop - 1],
            first_s.at[u, hop - 1], first_r.at[u, hop - 1], along(u, 0, k),
        )

    def start_plain(u, hop):
        prod[u][hop] = block(u, wrap(places(u)[0] + hop, 4))
        send_first(u, hop)

    def start_paired(u, hop):
        pair[u - 2, hop] = block_of(u, wrap(places(u)[0] + hop, 4), 1 - parity)
        sent_pair[u, hop] = push(
            pair.at[u - 2, hop], pair_in.at[u - 2, hop],
            pair_s.at[u - 2, hop], pair_r.at[u - 2, hop], mates[u],
        )

    for hop in (*HOPS, 0):
        for u in range(4):
            if hop == HOPS[0]:
                across[u].wait_recv()
                g_all[u][TOK : 2 * TOK, :] = g_recv[u][...].astype(jnp.bfloat16)
            if u in PAIRED:
                start_paired(u, hop)
            elif hop:
                start_plain(u, hop)
        if hop == HOPS[0]:
            pl.semaphore_wait(near1, 2)
            signal(near2, up(2), up(NZ - 2))
    for hop in (*HOPS, 0):
        for u in PAIRED:
            prod[u][hop] = block_of(u, wrap(places(u)[0] + hop, 4), parity)
    for u in PLAIN:
        prod[u][0] = block(u, places(u)[0])

    def cotangent(h):
        d_ref[:, h * 256 : (h + 1) * 256] = lax.dot_general(
            g_in[...], w_in[h * 256 : (h + 1) * 256, :], (((1,), (1,)), ((), ())),
            preferred_element_type=jnp.float32,
        ).astype(jnp.bfloat16)

    pl.semaphore_wait(near2, 2)
    signal(near4, up(4), up(NZ - 4))
    for hop in HOPS:
        for u in PAIRED:
            sent_pair[u, hop].wait_recv()
            prod[u][hop] = prod[u][hop] + pair_in[u - 2, hop]
            send_first(u, hop)

    loads[2].wait()
    for h in range(4):
        cotangent(h)
    pl.semaphore_wait(near4, 2)
    signal(near_twin, twin)

    def end_first(u):
        into = first_in if u in PLAIN else first_in_p
        if u in PAIRED:
            sent_pair[u, 0].wait_recv()
        for hop in (1, 3, 2):
            sent_first[u, hop].wait_recv()
        i = u % 2
        total = prod[u][0] + into[i, 0] + into[i, 1] + into[i, 2]
        if u in PAIRED:
            total = total + pair_in[u - 2, 0]
        prod[u][0] = total
        into = second_in if u in PLAIN else second_in_p
        for hop in HOPS:
            k = wrap(places(u)[1] + hop, 4)
            sent_second[u, hop] = push(
                prod[u].at[0, k], into.at[i, hop - 1],
                second_s.at[u, hop - 1], second_r.at[u, hop - 1], along(u, 1, k),
            )

    def end_second(u, zsend):
        into = second_in if u in PLAIN else second_in_p
        for hop in (1, 3, 2):
            sent_second[u, hop].wait_recv()
        i = u % 2
        total = prod[u][0, places(u)[1]] + into[i, 0] + into[i, 1] + into[i, 2]
        start = STARTS[u] - STARTS[u - i]
        for k in range(zsend.shape[0]):
            to = k if u in PAIRED else (k % 8 // 2 * 2 + k // 8) * 2 + k % 2
            zsend[to, :, start : start + WIDTHS[u]] = total[2 * k : 2 * k + 2]

    def along_z(zsend, zrecv, s, r, slot, near, count, z_of):
        for offset in sorted(range(count), key=lambda k: -min(k, count - k)):
            place = wrap(near + offset, count)
            z_ = z_of(place)
            for c_ in (core, 1 - core):
                k = place * 2 + c_
                if offset == 0 and c_ is core:
                    mine = z_ == z

                    @pl.when(jnp.logical_not(mine))
                    def _():
                        push(zsend.at[k], zrecv.at[slot], s, r, device(z_, y, x, c_))

                    @pl.when(mine)
                    def _():
                        pltpu.make_async_copy(zsend.at[k], zrecv.at[slot], r).start()
                else:
                    push(zsend.at[k], zrecv.at[slot], s, r, device(z_, y, x, c_))

    for u in PLAIN:
        end_first(u)
    for u in PAIRED:
        end_first(u)
    for u in PLAIN:
        end_second(u, zsend0)
    pl.semaphore_wait(near_twin, 1)
    along_z(
        zsend0, zrecv0, z0_s, z0_r, z, lax.rem(z, 8), 8, lambda place: 8 * core + place
    )
    for u in PAIRED:
        end_second(u, zsend1)
    along_z(
        zsend1, zrecv1, z1_s, z1_r, z // 2, lax.rem(z // 2, 4), 4,
        lambda place: 8 * core + 2 * place + parity,
    )

    def gather_z(zrecv, r):
        pltpu.make_async_copy(zrecv, zrecv, r).wait()
        total = zrecv[0]
        for k in range(1, zrecv.shape[0]):
            total = total + zrecv[k]
        return total

    def spill(part, tile):
        for p in range(2):
            for k in range(part.shape[1] // 128):
                at = p * 8 + tile + k
                result[at : at + 1, :] = part[p : p + 1, k * 128 : (k + 1) * 128]

    plain = gather_z(zrecv0, z0_r)
    spill(plain, 0)
    paired = gather_z(zrecv1, z1_r)
    spill(paired, WIDE0 // 128)

    def spread(slots, slot, targets, s, r, value):
        slots[slot] = value
        for target in targets:
            push(slots.at[slot], slots.at[slot], s, r, target)

    def collect(slots, count, r):
        arrived = slots.at[pl.ds(0, count)]
        pltpu.make_async_copy(arrived, arrived, r).wait()
        return jnp.sum(slots[...], axis=0)

    def left(buffer, count, s):
        gone = buffer.at[pl.ds(0, count)]
        pltpu.make_async_copy(gone, gone, s).wait()

    square = jnp.zeros((1, 128), jnp.float32)
    for part in (plain, paired):
        lanes = jnp.sum(part * part, axis=0, keepdims=True)
        for k in range(part.shape[1] // 128):
            square = square + lanes[:, k * 128 : (k + 1) * 128]
    away = [(j, i) for j in range(NY) for i in range(NX)]
    away.sort(key=lambda k: -min(k[0], NY - k[0]) - min(k[1], NX - k[1]))
    plane = [
        device(z, wrap(y + j, NY), wrap(x + i, NX), c_)
        for j, i in away for c_ in (1 - core, core) if j or i
    ] + [twin]
    spread(plane_sum, (y * NX + x) * 2 + core, plane, p_s, p_r, square)
    for sent in (across, sent_pair, sent_first):
        for copy in sent.values():
            copy.wait_send()
    square = collect(plane_sum, PLANE - 1, p_r)
    offsets = sorted(range(1, NZ), key=lambda k: -min(k, NZ - k))
    spread(ring_sum, z, [up(k) for k in offsets], q_s, q_r, square)
    for copy in sent_second.values():
        copy.wait_send()
    at_home = (z // 8) == core

    @pl.when(at_home)
    def _():
        left(zsend0, 15, z0_s)
        left(zsend1, 7, z1_s)

    @pl.when(jnp.logical_not(at_home))
    def _():
        left(zsend0, 16, z0_s)
        left(zsend1, 8, z1_s)

    left(plane_sum, PLANE - 1, p_s)
    result[16:17, :] = collect(ring_sum, NZ - 1, q_r)
    left(ring_sum, NZ - 1, q_s)


def update_kernel(
    d, result, cm, cv, ma, sm, sv, d_out, mu_out, vu_out, nm_out, mu, vu, nm, store_sem
):
    stores = [
        pltpu.make_async_copy(src, dst, store_sem.at[i])
        for i, (src, dst) in enumerate(((d, d_out), (mu, mu_out), (vu, vu_out), (nm, nm_out)))
    ]
    stores[0].start()
    squares = jnp.sum(result[16:17, :], axis=1, keepdims=True)
    clip = jnp.minimum(1.0, 1.0 / jnp.sqrt(squares + 1e-12))
    scale_m, scale_v = sm[0], sv[0]
    m_old = scale_m * (cm[...].astype(jnp.float32) - 127.0) / 127.0
    ratio_v = cv[...].astype(jnp.float32) / 255.0
    v_old = scale_v * ratio_v * ratio_v
    clipped = clip * result[0:16, :]
    m_new = 0.9 * m_old + 0.1 * clipped
    v_new = 0.95 * v_old + 0.05 * clipped * clipped
    update = m_new / (1.0 - 0.9**STEP) / (jnp.sqrt(v_new / (1.0 - 0.95**STEP)) + 1e-08)
    nm[...] = ma[...] - 0.01 * (update + 0.1 * ma[...])
    mu[...] = m_new / scale_m
    vu[...] = v_new / scale_v
    for store in stores[1:]:
        store.start()
    for store in stores:
        store.wait()


def local(attn_out, grad_out, w_out, codes_m, codes_v, scale_m, scale_v, master):
    f32, bf16 = jnp.float32, jnp.bfloat16
    vmem, dma = pltpu.VMEM, pltpu.SemaphoreType.DMA
    shape = jax.ShapeDtypeStruct
    near = pl.BlockSpec(memory_space=pltpu.VMEM)
    scalar = pl.BlockSpec(memory_space=pltpu.SMEM)
    hbm = pl.BlockSpec(memory_space=pltpu.HBM)
    block = shape((16, 128), f32)
    d_attn, result = pl.pallas_call(
        kernel,
        out_shape=(shape((TOK, 1024), bf16), shape((24, 128), f32)),
        in_specs=[hbm] * 3,
        out_specs=(near,) * 2,
        scratch_shapes=[
            vmem((TOK, 1024), bf16),
            vmem((TOK, 1024), bf16),
            vmem((1024, 1024), bf16),
            vmem((512, TOK), f32),
            vmem((512, TOK), f32),
            vmem((4, 4, 2, 16, 2 * TOK), bf16),
            *[vmem((TOK, w), f32) for w in WIDTHS],
            *[vmem((TOK, w), f32) for w in WIDTHS],
            *[vmem((2 * TOK, w), bf16) for w in WIDTHS],
            vmem((4, 4, 32, WIDTHS[0]), f32),
            vmem((4, 4, 32, WIDTHS[1]), f32),
            vmem((4, 4, 16, WIDTHS[2]), f32),
            vmem((4, 4, 16, WIDTHS[3]), f32),
            vmem((2, 4, 4, 16, WIDTHS[2]), f32),
            vmem((2, 4, 4, 16, WIDTHS[2]), f32),
            vmem((2, 3, 4, 32, WIDTHS[0]), f32),
            vmem((2, 3, 4, 16, WIDTHS[2]), f32),
            vmem((2, 3, 32, WIDTHS[0]), f32),
            vmem((2, 3, 16, WIDTHS[2]), f32),
            vmem((16, 2, WIDE0), f32),
            vmem((16, 2, WIDE0), f32),
            vmem((8, 2, WIDE1), f32),
            vmem((8, 2, WIDE1), f32),
            vmem((PLANE, 1, 128), f32),
            vmem((NZ, 1, 128), f32),
            dma((3,)),
            dma((5,)),
            dma((5,)),
            dma((2, 4)),
            dma((2, 4)),
            dma((4, 3)),
            dma((4, 3)),
            dma((4, 3)),
            dma((4, 3)),
            *[dma] * 8,
            vmem((512, 512), bf16),
            *[pltpu.SemaphoreType.REGULAR] * 4,
        ],
        compiler_params=pltpu.CompilerParams(
            collective_id=0, has_side_effects=True, vmem_limit_bytes=VMEM
        ),
        cost_estimate=pl.CostEstimate(
            flops=2 * 2 * TOK * 1024 * 1024, bytes_accessed=3 * 2**20, transcendentals=0
        ),
    )(attn_out, grad_out, w_out)
    d_attn, m_unit, v_unit, new_master = pl.pallas_call(
        update_kernel,
        out_shape=(shape((TOK, 1024), bf16), block, block, block),
        in_specs=[near] * 5 + [scalar] * 2,
        out_specs=(hbm,) * 4,
        scratch_shapes=[
            vmem((16, 128), f32),
            vmem((16, 128), f32),
            vmem((16, 128), f32),
            dma((4,)),
        ],
        compiler_params=pltpu.CompilerParams(vmem_limit_bytes=VMEM),
        cost_estimate=pl.CostEstimate(flops=2048 * 30, bytes_accessed=2**19, transcendentals=4096),
    )(
        d_attn, result, codes_m.reshape(16, 128), codes_v.reshape(16, 128),
        master.reshape(16, 128), scale_m, scale_v,
    )
    return (
        d_attn, m_unit.reshape(1, 2048), v_unit.reshape(1, 2048), new_master.reshape(1, 2048)
    )


def solution(mesh):
    in_specs = (
        P("dp", None),
        P("dp", None),
        P(),
        P("dp", None),
        P("dp", None),
        P("dp"),
        P("dp"),
        P("dp", None),
    )
    out_specs = (P("dp", None), P("dp", None), P("dp", None), P("dp", None))
    return jax.shard_map(local, mesh=mesh, in_specs=in_specs, out_specs=out_specs, check_vma=False)
```

```python
import functools

import jax
import jax.numpy as jnp
from jax import lax
from jax.experimental import pallas as pl
from jax.experimental.pallas import tpu as pltpu
from jax.sharding import PartitionSpec as P

STEP = 100
NX, NY, NZ = 4, 4, 16
PLANE = NX * NY * 2
TOK = 128
VMEM = int(53.5 * 2**20)
WIDTHS = (256, 256, 256, 256)
STARTS = tuple(sum(WIDTHS[:u]) for u in range(4))
PLAIN, PAIRED = (0, 1), (2, 3)
WIDE0, WIDE1 = WIDTHS[0] + WIDTHS[1], WIDTHS[2] + WIDTHS[3]
HOPS = (2, 1, 3)
MESH = pl.DeviceIdType.MESH


def push(src, dst, s, r, target):
    copy = pltpu.make_async_remote_copy(
        src_ref=src, dst_ref=dst, send_sem=s, recv_sem=r, device_id=(target,), device_id_type=MESH
    )
    copy.start()
    return copy


def wrap(value, n):
    return jnp.where(value >= n, value - n, value)


def kernel(
    a_hbm, g_hbm, w_hbm,
    d_ref, result,
    a_in, g_in, w_in,
    at_send, at_recv, at_all,
    gs0, gs1, gs2, gs3, gr0, gr1, gr2, gr3, ga0, ga1, ga2, ga3,
    prod0, prod1, prod2, prod3, pair, pair_in, first_in, first_in_p, second_in, second_in_p,
    zsend0, zrecv0, zsend1, zrecv1, plane_sum, ring_sum,
    in_sem, core_s, core_r, pair_s, pair_r, first_s, first_r, second_s, second_r,
    z0_s, z0_r, z1_s, z1_r, p_s, p_r, q_s, q_r,
    order, near1, near2, near4, near_twin,
):
    me = lax.axis_index("dp")
    core = lax.rem(me, 2)
    x = lax.rem(me // 2, NX)
    y = lax.rem(me // (2 * NX), NY)
    z = me // PLANE
    parity = lax.rem(z, 2)

    def device(z_, y_, x_, c_):
        return ((z_ * NY + y_) * NX + x_) * 2 + c_

    loads = []
    for i, (src, dst) in enumerate(((g_hbm, g_in), (a_hbm, a_in), (w_hbm, w_in))):
        copy = pltpu.make_async_copy(src, dst, in_sem.at[i])
        copy.start()
        loads.append(copy)

    def up(k):
        return device(wrap(z + k, NZ), y, x, core)

    def signal(semaphore, *targets):
        for target in targets:
            pl.semaphore_signal(
                semaphore, inc=1, device_id=(target,), device_id_type=MESH
            )

    twin = device(z, y, x, 1 - core)
    signal(
        pltpu.get_barrier_semaphore(), up(1), up(NZ - 1),
        *[device(z, y, wrap(x + k, NX), core) for k in HOPS],
        *[device(z, wrap(y + k, NY), x, core) for k in HOPS],
        twin,
    )

    row = lax.broadcasted_iota(jnp.int32, (512, 512), 0)
    column = lax.broadcasted_iota(jnp.int32, (512, 512), 1)
    wanted = (
        ((row >> 2) & 3) * 128
        + ((row >> 4) & 1) * 64
        + ((row >> 5) & 3) * 16
        + ((row >> 7) & 3) * 4
        + (row & 3)
    )
    order[...] = jnp.where(wanted == column, 1.0, 0.0).astype(jnp.bfloat16)

    def rows_of(c_):
        half = a_in[:, pl.ds(pl.multiple_of(c_ * 512, 512), 512)]
        return lax.dot_general(
            order[...], half, (((1,), (1,)), ((), ())), preferred_element_type=jnp.float32
        )

    g_send, g_recv, g_all = (gs0, gs1, gs2, gs3), (gr0, gr1, gr2, gr3), (ga0, ga1, ga2, ga3)
    across = {}

    def cross(u):
        piece = g_in[:, STARTS[u] : STARTS[u] + WIDTHS[u]]
        g_send[u][...] = piece.astype(jnp.float32)
        if u == 0:
            pl.semaphore_wait(pltpu.get_barrier_semaphore(), 9)
        across[u] = push(g_send[u], g_recv[u], core_s.at[u], core_r.at[u], twin)
        g_all[u][0:TOK, :] = piece

    loads[0].wait()
    cross(0)
    loads[1].wait()
    at_send[...] = rows_of(1 - core)
    across[4] = push(at_send, at_recv, core_s.at[4], core_r.at[4], twin)
    for u in range(1, 4):
        cross(u)
    signal(near1, up(1), up(NZ - 1))

    at_all[:, :, :, :, 0:TOK] = rows_of(core).astype(jnp.bfloat16).reshape(4, 4, 2, 16, TOK)
    across[4].wait_recv()
    at_all[:, :, :, :, TOK : 2 * TOK] = (
        at_recv[...].astype(jnp.bfloat16).reshape(4, 4, 2, 16, TOK)
    )

    def times(rows, u):
        return jnp.dot(rows, g_all[u][...], preferred_element_type=jnp.float32)

    def block(u, k):
        rows = at_all[k] if u % 2 == 0 else at_all[:, k]
        return times(rows.reshape(128, 2 * TOK), u).reshape(4, 32, WIDTHS[u])

    def block_of(u, k, parity_):
        rows = at_all[k, :, parity_] if u % 2 == 0 else at_all[:, k, parity_]
        return times(rows.reshape(64, 2 * TOK), u).reshape(4, 16, WIDTHS[u])

    def places(u):
        return (x, y) if u % 2 == 0 else (y, x)

    def along(u, stage, k):
        if (u % 2 == 0) == (stage == 0):
            return device(z, y, k, core)
        return device(z, k, x, core)

    prod = (prod0, prod1, prod2, prod3)
    odd = parity == 1
    mates = {
        2: jnp.where(odd, up(NZ - 1), up(1)),
        3: jnp.where(odd, up(1), up(NZ - 1)),
    }
    sent_pair, sent_first, sent_second = {}, {}, {}

    def send_first(u, hop):
        k = wrap(places(u)[0] + hop, 4)
        into = first_in if u in PLAIN else first_in_p
        sent_first[u, hop] = push(
            prod[u].at[hop], into.at[u % 2, hop - 1],
            first_s.at[u, hop - 1], first_r.at[u, hop - 1], along(u, 0, k),
        )

    def start_plain(u, hop):
        prod[u][hop] = block(u, wrap(places(u)[0] + hop, 4))
        send_first(u, hop)

    def start_paired(u, hop):
        pair[u - 2, hop] = block_of(u, wrap(places(u)[0] + hop, 4), 1 - parity)
        sent_pair[u, hop] = push(
            pair.at[u - 2, hop], pair_in.at[u - 2, hop],
            pair_s.at[u - 2, hop], pair_r.at[u - 2, hop], mates[u],
        )

    for hop in (*HOPS, 0):
        for u in range(4):
            if hop == HOPS[0]:
                across[u].wait_recv()
                g_all[u][TOK : 2 * TOK, :] = g_recv[u][...].astype(jnp.bfloat16)
            if u in PAIRED:
                start_paired(u, hop)
            elif hop:
                start_plain(u, hop)
        if hop == HOPS[0]:
            pl.semaphore_wait(near1, 2)
            signal(near2, up(2), up(NZ - 2))
    for hop in (*HOPS, 0):
        for u in PAIRED:
            prod[u][hop] = block_of(u, wrap(places(u)[0] + hop, 4), parity)
    for u in PLAIN:
        prod[u][0] = block(u, places(u)[0])

    def cotangent(h):
        d_ref[:, h * 256 : (h + 1) * 256] = lax.dot_general(
            g_in[...], w_in[h * 256 : (h + 1) * 256, :], (((1,), (1,)), ((), ())),
            preferred_element_type=jnp.float32,
        ).astype(jnp.bfloat16)

    pl.semaphore_wait(near2, 2)
    signal(near4, up(4), up(NZ - 4))
    for hop in HOPS:
        for u in PAIRED:
            sent_pair[u, hop].wait_recv()
            prod[u][hop] = prod[u][hop] + pair_in[u - 2, hop]
            send_first(u, hop)


    def end_first(u):
        into = first_in if u in PLAIN else first_in_p
        if u in PAIRED:
            sent_pair[u, 0].wait_recv()
        for hop in (1, 3, 2):
            sent_first[u, hop].wait_recv()
        i = u % 2
        total = prod[u][0] + into[i, 0] + into[i, 1] + into[i, 2]
        if u in PAIRED:
            total = total + pair_in[u - 2, 0]
        prod[u][0] = total
        into = second_in if u in PLAIN else second_in_p
        for hop in HOPS:
            k = wrap(places(u)[1] + hop, 4)
            sent_second[u, hop] = push(
                prod[u].at[0, k], into.at[i, hop - 1],
                second_s.at[u, hop - 1], second_r.at[u, hop - 1], along(u, 1, k),
            )

    def end_second(u, zsend):
        into = second_in if u in PLAIN else second_in_p
        for hop in (1, 3, 2):
            sent_second[u, hop].wait_recv()
        i = u % 2
        total = prod[u][0, places(u)[1]] + into[i, 0] + into[i, 1] + into[i, 2]
        start = STARTS[u] - STARTS[u - i]
        for k in range(zsend.shape[0]):
            to = k if u in PAIRED else (k % 8 // 2 * 2 + k // 8) * 2 + k % 2
            zsend[to, :, start : start + WIDTHS[u]] = total[2 * k : 2 * k + 2]

    def along_z(zsend, zrecv, s, r, slot, near, count, z_of):
        for offset in sorted(range(count), key=lambda k: -min(k, count - k)):
            place = wrap(near + offset, count)
            z_ = z_of(place)
            for c_ in (core, 1 - core):
                k = place * 2 + c_
                if offset == 0 and c_ is core:
                    mine = z_ == z

                    @pl.when(jnp.logical_not(mine))
                    def _():
                        push(zsend.at[k], zrecv.at[slot], s, r, device(z_, y, x, c_))

                    @pl.when(mine)
                    def _():
                        pltpu.make_async_copy(zsend.at[k], zrecv.at[slot], r).start()
                else:
                    push(zsend.at[k], zrecv.at[slot], s, r, device(z_, y, x, c_))

    for u in PLAIN:
        end_first(u)
    pl.semaphore_wait(near4, 2)
    signal(near_twin, twin)
    for u in PAIRED:
        end_first(u)
    for u in PLAIN:
        end_second(u, zsend0)
    pl.semaphore_wait(near_twin, 1)
    along_z(
        zsend0, zrecv0, z0_s, z0_r, z, lax.rem(z, 8), 8, lambda place: 8 * core + place
    )
    for u in PAIRED:
        end_second(u, zsend1)
    along_z(
        zsend1, zrecv1, z1_s, z1_r, z // 2, lax.rem(z // 2, 4), 4,
        lambda place: 8 * core + 2 * place + parity,
    )

    def gather_z(zrecv, r):
        pltpu.make_async_copy(zrecv, zrecv, r).wait()
        total = zrecv[0]
        for k in range(1, zrecv.shape[0]):
            total = total + zrecv[k]
        return total

    def spill(part, tile):
        for p in range(2):
            for k in range(part.shape[1] // 128):
                at = p * 8 + tile + k
                result[at : at + 1, :] = part[p : p + 1, k * 128 : (k + 1) * 128]

    plain = gather_z(zrecv0, z0_r)
    spill(plain, 0)
    paired = gather_z(zrecv1, z1_r)
    spill(paired, WIDE0 // 128)

    def spread(slots, slot, targets, s, r, value):
        slots[slot] = value
        for target in targets:
            push(slots.at[slot], slots.at[slot], s, r, target)

    def collect(slots, count, r):
        arrived = slots.at[pl.ds(0, count)]
        pltpu.make_async_copy(arrived, arrived, r).wait()
        return jnp.sum(slots[...], axis=0)

    def left(buffer, count, s):
        gone = buffer.at[pl.ds(0, count)]
        pltpu.make_async_copy(gone, gone, s).wait()

    square = jnp.zeros((1, 128), jnp.float32)
    for part in (plain, paired):
        lanes = jnp.sum(part * part, axis=0, keepdims=True)
        for k in range(part.shape[1] // 128):
            square = square + lanes[:, k * 128 : (k + 1) * 128]
    away = [(j, i) for j in range(NY) for i in range(NX)]
    away.sort(key=lambda k: -min(k[0], NY - k[0]) - min(k[1], NX - k[1]))
    plane = [
        device(z, wrap(y + j, NY), wrap(x + i, NX), c_)
        for j, i in away for c_ in (1 - core, core) if j or i
    ] + [twin]
    spread(plane_sum, (y * NX + x) * 2 + core, plane, p_s, p_r, square)
    for sent in (across, sent_pair, sent_first):
        for copy in sent.values():
            copy.wait_send()
    square = collect(plane_sum, PLANE - 1, p_r)
    offsets = sorted(range(1, NZ), key=lambda k: -min(k, NZ - k))
    spread(ring_sum, z, [up(k) for k in offsets], q_s, q_r, square)
    loads[2].wait()
    for h in range(4):
        cotangent(h)
    for copy in sent_second.values():
        copy.wait_send()
    at_home = (z // 8) == core

    @pl.when(at_home)
    def _():
        left(zsend0, 15, z0_s)
        left(zsend1, 7, z1_s)

    @pl.when(jnp.logical_not(at_home))
    def _():
        left(zsend0, 16, z0_s)
        left(zsend1, 8, z1_s)

    left(plane_sum, PLANE - 1, p_s)
    result[16:17, :] = collect(ring_sum, NZ - 1, q_r)
    left(ring_sum, NZ - 1, q_s)


def update_kernel(
    d, result, cm, cv, ma, sm, sv, d_out, mu_out, vu_out, nm_out, mu, vu, nm, store_sem
):
    stores = [
        pltpu.make_async_copy(src, dst, store_sem.at[i])
        for i, (src, dst) in enumerate(((d, d_out), (mu, mu_out), (vu, vu_out), (nm, nm_out)))
    ]
    stores[0].start()
    squares = jnp.sum(result[16:17, :], axis=1, keepdims=True)
    clip = jnp.minimum(1.0, 1.0 / jnp.sqrt(squares + 1e-12))
    scale_m, scale_v = sm[0], sv[0]
    m_old = scale_m * (cm[...].astype(jnp.float32) - 127.0) / 127.0
    ratio_v = cv[...].astype(jnp.float32) / 255.0
    v_old = scale_v * ratio_v * ratio_v
    clipped = clip * result[0:16, :]
    m_new = 0.9 * m_old + 0.1 * clipped
    v_new = 0.95 * v_old + 0.05 * clipped * clipped
    update = m_new / (1.0 - 0.9**STEP) / (jnp.sqrt(v_new / (1.0 - 0.95**STEP)) + 1e-08)
    nm[...] = ma[...] - 0.01 * (update + 0.1 * ma[...])
    mu[...] = m_new / scale_m
    vu[...] = v_new / scale_v
    for store in stores[1:]:
        store.start()
    for store in stores:
        store.wait()


def local(attn_out, grad_out, w_out, codes_m, codes_v, scale_m, scale_v, master):
    f32, bf16 = jnp.float32, jnp.bfloat16
    vmem, dma = pltpu.VMEM, pltpu.SemaphoreType.DMA
    shape = jax.ShapeDtypeStruct
    near = pl.BlockSpec(memory_space=pltpu.VMEM)
    scalar = pl.BlockSpec(memory_space=pltpu.SMEM)
    hbm = pl.BlockSpec(memory_space=pltpu.HBM)
    block = shape((16, 128), f32)
    d_attn, result = pl.pallas_call(
        kernel,
        out_shape=(shape((TOK, 1024), bf16), shape((24, 128), f32)),
        in_specs=[hbm] * 3,
        out_specs=(near,) * 2,
        scratch_shapes=[
            vmem((TOK, 1024), bf16),
            vmem((TOK, 1024), bf16),
            vmem((1024, 1024), bf16),
            vmem((512, TOK), f32),
            vmem((512, TOK), f32),
            vmem((4, 4, 2, 16, 2 * TOK), bf16),
            *[vmem((TOK, w), f32) for w in WIDTHS],
            *[vmem((TOK, w), f32) for w in WIDTHS],
            *[vmem((2 * TOK, w), bf16) for w in WIDTHS],
            vmem((4, 4, 32, WIDTHS[0]), f32),
            vmem((4, 4, 32, WIDTHS[1]), f32),
            vmem((4, 4, 16, WIDTHS[2]), f32),
            vmem((4, 4, 16, WIDTHS[3]), f32),
            vmem((2, 4, 4, 16, WIDTHS[2]), f32),
            vmem((2, 4, 4, 16, WIDTHS[2]), f32),
            vmem((2, 3, 4, 32, WIDTHS[0]), f32),
            vmem((2, 3, 4, 16, WIDTHS[2]), f32),
            vmem((2, 3, 32, WIDTHS[0]), f32),
            vmem((2, 3, 16, WIDTHS[2]), f32),
            vmem((16, 2, WIDE0), f32),
            vmem((16, 2, WIDE0), f32),
            vmem((8, 2, WIDE1), f32),
            vmem((8, 2, WIDE1), f32),
            vmem((PLANE, 1, 128), f32),
            vmem((NZ, 1, 128), f32),
            dma((3,)),
            dma((5,)),
            dma((5,)),
            dma((2, 4)),
            dma((2, 4)),
            dma((4, 3)),
            dma((4, 3)),
            dma((4, 3)),
            dma((4, 3)),
            *[dma] * 8,
            vmem((512, 512), bf16),
            *[pltpu.SemaphoreType.REGULAR] * 4,
        ],
        compiler_params=pltpu.CompilerParams(
            collective_id=0, has_side_effects=True, vmem_limit_bytes=VMEM
        ),
        cost_estimate=pl.CostEstimate(
            flops=2 * 2 * TOK * 1024 * 1024, bytes_accessed=3 * 2**20, transcendentals=0
        ),
    )(attn_out, grad_out, w_out)
    d_attn, m_unit, v_unit, new_master = pl.pallas_call(
        update_kernel,
        out_shape=(shape((TOK, 1024), bf16), block, block, block),
        in_specs=[near] * 5 + [scalar] * 2,
        out_specs=(hbm,) * 4,
        scratch_shapes=[
            vmem((16, 128), f32),
            vmem((16, 128), f32),
            vmem((16, 128), f32),
            dma((4,)),
        ],
        compiler_params=pltpu.CompilerParams(vmem_limit_bytes=VMEM),
        cost_estimate=pl.CostEstimate(flops=2048 * 30, bytes_accessed=2**19, transcendentals=4096),
    )(
        d_attn, result, codes_m.reshape(16, 128), codes_v.reshape(16, 128),
        master.reshape(16, 128), scale_m, scale_v,
    )
    return (
        d_attn, m_unit.reshape(1, 2048), v_unit.reshape(1, 2048), new_master.reshape(1, 2048)
    )


def solution(mesh):
    in_specs = (
        P("dp", None),
        P("dp", None),
        P(),
        P("dp", None),
        P("dp", None),
        P("dp"),
        P("dp"),
        P("dp", None),
    )
    out_specs = (P("dp", None), P("dp", None), P("dp", None), P("dp", None))
    return jax.shard_map(local, mesh=mesh, in_specs=in_specs, out_specs=out_specs, check_vma=False)
```

```python
import functools

import jax
import jax.numpy as jnp
from jax import lax
from jax.experimental import pallas as pl
from jax.experimental.pallas import tpu as pltpu
from jax.sharding import PartitionSpec as P

STEP = 100
NX, NY, NZ = 4, 4, 16
PLANE = NX * NY * 2
TOK = 128
VMEM = int(53.5 * 2**20)
WIDTHS = (256, 256, 256, 256)
STARTS = tuple(sum(WIDTHS[:u]) for u in range(4))
PLAIN, PAIRED = (0, 1), (2, 3)
WIDE0, WIDE1 = WIDTHS[0] + WIDTHS[1], WIDTHS[2] + WIDTHS[3]
HOPS = (2, 1, 3)
MESH = pl.DeviceIdType.MESH


def push(src, dst, s, r, target):
    copy = pltpu.make_async_remote_copy(
        src_ref=src, dst_ref=dst, send_sem=s, recv_sem=r, device_id=(target,), device_id_type=MESH
    )
    copy.start()
    return copy


def wrap(value, n):
    return jnp.where(value >= n, value - n, value)


def kernel(
    a_hbm, g_hbm, w_hbm,
    d_ref, result,
    a_in, g_in, w_in,
    at_send, at_recv, at_all,
    gs0, gs1, gs2, gs3, gr0, gr1, gr2, gr3, ga0, ga1, ga2, ga3,
    prod0, prod1, prod2, prod3, pair, pair_in, first_in, first_in_p, second_in, second_in_p,
    zsend0, zrecv0, zsend1, zrecv1, plane_sum, ring_sum,
    in_sem, core_s, core_r, pair_s, pair_r, first_s, first_r, second_s, second_r,
    z0_s, z0_r, z1_s, z1_r, p_s, p_r, q_s, q_r,
    order, near1, near2, near4, near_twin,
):
    me = lax.axis_index("dp")
    core = lax.rem(me, 2)
    x = lax.rem(me // 2, NX)
    y = lax.rem(me // (2 * NX), NY)
    z = me // PLANE
    parity = lax.rem(z, 2)

    def device(z_, y_, x_, c_):
        return ((z_ * NY + y_) * NX + x_) * 2 + c_

    loads = []
    for i, (src, dst) in enumerate(((g_hbm, g_in), (a_hbm, a_in), (w_hbm, w_in))):
        copy = pltpu.make_async_copy(src, dst, in_sem.at[i])
        copy.start()
        loads.append(copy)

    def up(k):
        return device(wrap(z + k, NZ), y, x, core)

    def signal(semaphore, *targets):
        for target in targets:
            pl.semaphore_signal(
                semaphore, inc=1, device_id=(target,), device_id_type=MESH
            )

    twin = device(z, y, x, 1 - core)
    signal(
        pltpu.get_barrier_semaphore(), up(1), up(NZ - 1),
        *[device(z, y, wrap(x + k, NX), core) for k in HOPS],
        *[device(z, wrap(y + k, NY), x, core) for k in HOPS],
        twin,
    )

    row = lax.broadcasted_iota(jnp.int32, (512, 512), 0)
    column = lax.broadcasted_iota(jnp.int32, (512, 512), 1)
    wanted = (
        ((row >> 2) & 3) * 128
        + ((row >> 4) & 1) * 64
        + ((row >> 5) & 3) * 16
        + ((row >> 7) & 3) * 4
        + (row & 3)
    )
    order[...] = jnp.where(wanted == column, 1.0, 0.0).astype(jnp.bfloat16)

    def rows_of(c_):
        half = a_in[:, pl.ds(pl.multiple_of(c_ * 512, 512), 512)]
        return lax.dot_general(
            order[...], half, (((1,), (1,)), ((), ())), preferred_element_type=jnp.float32
        )

    g_send, g_recv, g_all = (gs0, gs1, gs2, gs3), (gr0, gr1, gr2, gr3), (ga0, ga1, ga2, ga3)
    across = {}

    def cross(u):
        piece = g_in[:, STARTS[u] : STARTS[u] + WIDTHS[u]]
        g_send[u][...] = piece.astype(jnp.float32)
        if u == 0:
            pl.semaphore_wait(pltpu.get_barrier_semaphore(), 9)
        across[u] = push(g_send[u], g_recv[u], core_s.at[u], core_r.at[u], twin)
        g_all[u][0:TOK, :] = piece

    loads[0].wait()
    cross(0)
    loads[1].wait()
    at_send[...] = rows_of(1 - core)
    across[4] = push(at_send, at_recv, core_s.at[4], core_r.at[4], twin)
    for u in range(1, 4):
        cross(u)
    signal(near1, up(1), up(NZ - 1))

    at_all[:, :, :, :, 0:TOK] = rows_of(core).astype(jnp.bfloat16).reshape(4, 4, 2, 16, TOK)
    across[4].wait_recv()
    at_all[:, :, :, :, TOK : 2 * TOK] = (
        at_recv[...].astype(jnp.bfloat16).reshape(4, 4, 2, 16, TOK)
    )

    def times(rows, u):
        return jnp.dot(rows, g_all[u][...], preferred_element_type=jnp.float32)

    def block(u, k):
        rows = at_all[k] if u % 2 == 0 else at_all[:, k]
        return times(rows.reshape(128, 2 * TOK), u).reshape(4, 32, WIDTHS[u])

    def block_of(u, k, parity_):
        rows = at_all[k, :, parity_] if u % 2 == 0 else at_all[:, k, parity_]
        return times(rows.reshape(64, 2 * TOK), u).reshape(4, 16, WIDTHS[u])

    def places(u):
        return (x, y) if u % 2 == 0 else (y, x)

    def along(u, stage, k):
        if (u % 2 == 0) == (stage == 0):
            return device(z, y, k, core)
        return device(z, k, x, core)

    prod = (prod0, prod1, prod2, prod3)
    odd = parity == 1
    mates = {
        2: jnp.where(odd, up(NZ - 1), up(1)),
        3: jnp.where(odd, up(1), up(NZ - 1)),
    }
    sent_pair, sent_first, sent_second = {}, {}, {}

    def send_first(u, hop):
        k = wrap(places(u)[0] + hop, 4)
        into = first_in if u in PLAIN else first_in_p
        sent_first[u, hop] = push(
            prod[u].at[hop], into.at[u % 2, hop - 1],
            first_s.at[u, hop - 1], first_r.at[u, hop - 1], along(u, 0, k),
        )

    def start_plain(u, hop):
        prod[u][hop] = block(u, wrap(places(u)[0] + hop, 4))
        send_first(u, hop)

    def start_paired(u, hop):
        pair[u - 2, hop] = block_of(u, wrap(places(u)[0] + hop, 4), 1 - parity)
        sent_pair[u, hop] = push(
            pair.at[u - 2, hop], pair_in.at[u - 2, hop],
            pair_s.at[u - 2, hop], pair_r.at[u - 2, hop], mates[u],
        )

    for hop in (*HOPS, 0):
        for u in range(4):
            if hop == HOPS[0]:
                across[u].wait_recv()
                g_all[u][TOK : 2 * TOK, :] = g_recv[u][...].astype(jnp.bfloat16)
            if u in PAIRED:
                start_paired(u, hop)
            elif hop:
                start_plain(u, hop)
        if hop == HOPS[0]:
            pl.semaphore_wait(near1, 2)
            signal(near2, up(2), up(NZ - 2))
    for hop in (*HOPS, 0):
        for u in PAIRED:
            prod[u][hop] = block_of(u, wrap(places(u)[0] + hop, 4), parity)
    for u in PLAIN:
        prod[u][0] = block(u, places(u)[0])

    def cotangent(h):
        d_ref[:, h * 256 : (h + 1) * 256] = lax.dot_general(
            g_in[...], w_in[h * 256 : (h + 1) * 256, :], (((1,), (1,)), ((), ())),
            preferred_element_type=jnp.float32,
        ).astype(jnp.bfloat16)

    pl.semaphore_wait(near2, 2)
    signal(near4, up(4), up(NZ - 4))
    for hop in HOPS:
        for u in PAIRED:
            sent_pair[u, hop].wait_recv()
            prod[u][hop] = prod[u][hop] + pair_in[u - 2, hop]
            send_first(u, hop)


    def end_first(u):
        into = first_in if u in PLAIN else first_in_p
        if u in PAIRED:
            sent_pair[u, 0].wait_recv()
        for hop in (1, 3, 2):
            sent_first[u, hop].wait_recv()
        i = u % 2
        total = prod[u][0] + into[i, 0] + into[i, 1] + into[i, 2]
        if u in PAIRED:
            total = total + pair_in[u - 2, 0]
        prod[u][0] = total
        into = second_in if u in PLAIN else second_in_p
        for hop in HOPS:
            k = wrap(places(u)[1] + hop, 4)
            sent_second[u, hop] = push(
                prod[u].at[0, k], into.at[i, hop - 1],
                second_s.at[u, hop - 1], second_r.at[u, hop - 1], along(u, 1, k),
            )

    def end_second(u, zsend):
        into = second_in if u in PLAIN else second_in_p
        for hop in (1, 3, 2):
            sent_second[u, hop].wait_recv()
        i = u % 2
        total = prod[u][0, places(u)[1]] + into[i, 0] + into[i, 1] + into[i, 2]
        start = STARTS[u] - STARTS[u - i]
        for k in range(zsend.shape[0]):
            to = k if u in PAIRED else (k % 8 // 2 * 2 + k // 8) * 2 + k % 2
            zsend[to, :, start : start + WIDTHS[u]] = total[2 * k : 2 * k + 2]

    def along_z(zsend, zrecv, s, r, slot, near, count, z_of):
        for offset in sorted(range(count), key=lambda k: -min(k, count - k)):
            place = wrap(near + offset, count)
            z_ = z_of(place)
            for c_ in (core, 1 - core):
                k = place * 2 + c_
                if offset == 0 and c_ is core:
                    mine = z_ == z

                    @pl.when(jnp.logical_not(mine))
                    def _():
                        push(zsend.at[k], zrecv.at[slot], s, r, device(z_, y, x, c_))

                    @pl.when(mine)
                    def _():
                        pltpu.make_async_copy(zsend.at[k], zrecv.at[slot], r).start()
                else:
                    push(zsend.at[k], zrecv.at[slot], s, r, device(z_, y, x, c_))

    for u in PLAIN:
        end_first(u)
    pl.semaphore_wait(near4, 2)
    signal(near_twin, twin)
    for u in PAIRED:
        end_first(u)
    for u in PLAIN:
        end_second(u, zsend0)
    pl.semaphore_wait(near_twin, 1)
    along_z(
        zsend0, zrecv0, z0_s, z0_r, z, lax.rem(z, 8), 8, lambda place: 8 * core + place
    )
    for u in PAIRED:
        end_second(u, zsend1)
    along_z(
        zsend1, zrecv1, z1_s, z1_r, z // 2, lax.rem(z // 2, 4), 4,
        lambda place: 8 * core + 2 * place + parity,
    )

    def gather_z(zrecv, r):
        pltpu.make_async_copy(zrecv, zrecv, r).wait()
        total = zrecv[0]
        for k in range(1, zrecv.shape[0]):
            total = total + zrecv[k]
        return total

    def spill(part, tile):
        for p in range(2):
            for k in range(part.shape[1] // 128):
                at = p * 8 + tile + k
                result[at : at + 1, :] = part[p : p + 1, k * 128 : (k + 1) * 128]

    plain = gather_z(zrecv0, z0_r)
    spill(plain, 0)
    def squares_of(part):
        lanes = jnp.sum(part * part, axis=0, keepdims=True)
        return sum(lanes[:, k * 128 : (k + 1) * 128] for k in range(part.shape[1] // 128))

    square = squares_of(plain)
    paired = gather_z(zrecv1, z1_r)

    def spread(slots, slot, targets, s, r, value):
        slots[slot] = value
        for target in targets:
            push(slots.at[slot], slots.at[slot], s, r, target)

    def collect(slots, count, r):
        arrived = slots.at[pl.ds(0, count)]
        pltpu.make_async_copy(arrived, arrived, r).wait()
        return jnp.sum(slots[...], axis=0)

    def left(buffer, count, s):
        gone = buffer.at[pl.ds(0, count)]
        pltpu.make_async_copy(gone, gone, s).wait()

    square = square + squares_of(paired)
    away = [(j, i) for j in range(NY) for i in range(NX)]
    away.sort(key=lambda k: -min(k[0], NY - k[0]) - min(k[1], NX - k[1]))
    plane = [
        device(z, wrap(y + j, NY), wrap(x + i, NX), c_)
        for j, i in away for c_ in (1 - core, core) if j or i
    ] + [twin]
    spread(plane_sum, (y * NX + x) * 2 + core, plane, p_s, p_r, square)
    spill(paired, WIDE0 // 128)
    for sent in (across, sent_pair, sent_first):
        for copy in sent.values():
            copy.wait_send()
    square = collect(plane_sum, PLANE - 1, p_r)
    offsets = sorted(range(1, NZ), key=lambda k: -min(k, NZ - k))
    spread(ring_sum, z, [up(k) for k in offsets], q_s, q_r, square)
    loads[2].wait()
    for h in range(4):
        cotangent(h)
    for copy in sent_second.values():
        copy.wait_send()
    at_home = (z // 8) == core

    @pl.when(at_home)
    def _():
        left(zsend0, 15, z0_s)
        left(zsend1, 7, z1_s)

    @pl.when(jnp.logical_not(at_home))
    def _():
        left(zsend0, 16, z0_s)
        left(zsend1, 8, z1_s)

    left(plane_sum, PLANE - 1, p_s)
    result[16:17, :] = collect(ring_sum, NZ - 1, q_r)
    left(ring_sum, NZ - 1, q_s)


def update_kernel(
    d, result, cm, cv, ma, sm, sv, d_out, mu_out, vu_out, nm_out, mu, vu, nm, store_sem
):
    stores = [
        pltpu.make_async_copy(src, dst, store_sem.at[i])
        for i, (src, dst) in enumerate(((d, d_out), (mu, mu_out), (vu, vu_out), (nm, nm_out)))
    ]
    stores[0].start()
    squares = jnp.sum(result[16:17, :], axis=1, keepdims=True)
    clip = jnp.minimum(1.0, 1.0 / jnp.sqrt(squares + 1e-12))
    scale_m, scale_v = sm[0], sv[0]
    m_old = scale_m * (cm[...].astype(jnp.float32) - 127.0) / 127.0
    ratio_v = cv[...].astype(jnp.float32) / 255.0
    v_old = scale_v * ratio_v * ratio_v
    clipped = clip * result[0:16, :]
    m_new = 0.9 * m_old + 0.1 * clipped
    v_new = 0.95 * v_old + 0.05 * clipped * clipped
    update = m_new / (1.0 - 0.9**STEP) / (jnp.sqrt(v_new / (1.0 - 0.95**STEP)) + 1e-08)
    nm[...] = ma[...] - 0.01 * (update + 0.1 * ma[...])
    mu[...] = m_new / scale_m
    vu[...] = v_new / scale_v
    for store in stores[1:]:
        store.start()
    for store in stores:
        store.wait()


def local(attn_out, grad_out, w_out, codes_m, codes_v, scale_m, scale_v, master):
    f32, bf16 = jnp.float32, jnp.bfloat16
    vmem, dma = pltpu.VMEM, pltpu.SemaphoreType.DMA
    shape = jax.ShapeDtypeStruct
    near = pl.BlockSpec(memory_space=pltpu.VMEM)
    scalar = pl.BlockSpec(memory_space=pltpu.SMEM)
    hbm = pl.BlockSpec(memory_space=pltpu.HBM)
    block = shape((16, 128), f32)
    d_attn, result = pl.pallas_call(
        kernel,
        out_shape=(shape((TOK, 1024), bf16), shape((24, 128), f32)),
        in_specs=[hbm] * 3,
        out_specs=(near,) * 2,
        scratch_shapes=[
            vmem((TOK, 1024), bf16),
            vmem((TOK, 1024), bf16),
            vmem((1024, 1024), bf16),
            vmem((512, TOK), f32),
            vmem((512, TOK), f32),
            vmem((4, 4, 2, 16, 2 * TOK), bf16),
            *[vmem((TOK, w), f32) for w in WIDTHS],
            *[vmem((TOK, w), f32) for w in WIDTHS],
            *[vmem((2 * TOK, w), bf16) for w in WIDTHS],
            vmem((4, 4, 32, WIDTHS[0]), f32),
            vmem((4, 4, 32, WIDTHS[1]), f32),
            vmem((4, 4, 16, WIDTHS[2]), f32),
            vmem((4, 4, 16, WIDTHS[3]), f32),
            vmem((2, 4, 4, 16, WIDTHS[2]), f32),
            vmem((2, 4, 4, 16, WIDTHS[2]), f32),
            vmem((2, 3, 4, 32, WIDTHS[0]), f32),
            vmem((2, 3, 4, 16, WIDTHS[2]), f32),
            vmem((2, 3, 32, WIDTHS[0]), f32),
            vmem((2, 3, 16, WIDTHS[2]), f32),
            vmem((16, 2, WIDE0), f32),
            vmem((16, 2, WIDE0), f32),
            vmem((8, 2, WIDE1), f32),
            vmem((8, 2, WIDE1), f32),
            vmem((PLANE, 1, 128), f32),
            vmem((NZ, 1, 128), f32),
            dma((3,)),
            dma((5,)),
            dma((5,)),
            dma((2, 4)),
            dma((2, 4)),
            dma((4, 3)),
            dma((4, 3)),
            dma((4, 3)),
            dma((4, 3)),
            *[dma] * 8,
            vmem((512, 512), bf16),
            *[pltpu.SemaphoreType.REGULAR] * 4,
        ],
        compiler_params=pltpu.CompilerParams(
            collective_id=0, has_side_effects=True, vmem_limit_bytes=VMEM
        ),
        cost_estimate=pl.CostEstimate(
            flops=2 * 2 * TOK * 1024 * 1024, bytes_accessed=3 * 2**20, transcendentals=0
        ),
    )(attn_out, grad_out, w_out)
    d_attn, m_unit, v_unit, new_master = pl.pallas_call(
        update_kernel,
        out_shape=(shape((TOK, 1024), bf16), block, block, block),
        in_specs=[near] * 5 + [scalar] * 2,
        out_specs=(hbm,) * 4,
        scratch_shapes=[
            vmem((16, 128), f32),
            vmem((16, 128), f32),
            vmem((16, 128), f32),
            dma((4,)),
        ],
        compiler_params=pltpu.CompilerParams(vmem_limit_bytes=VMEM),
        cost_estimate=pl.CostEstimate(flops=2048 * 30, bytes_accessed=2**19, transcendentals=4096),
    )(
        d_attn, result, codes_m.reshape(16, 128), codes_v.reshape(16, 128),
        master.reshape(16, 128), scale_m, scale_v,
    )
    return (
        d_attn, m_unit.reshape(1, 2048), v_unit.reshape(1, 2048), new_master.reshape(1, 2048)
    )


def solution(mesh):
    in_specs = (
        P("dp", None),
        P("dp", None),
        P(),
        P("dp", None),
        P("dp", None),
        P("dp"),
        P("dp"),
        P("dp", None),
    )
    out_specs = (P("dp", None), P("dp", None), P("dp", None), P("dp", None))
    return jax.shard_map(local, mesh=mesh, in_specs=in_specs, out_specs=out_specs, check_vma=False)
```
